256 devices in a mesh: tm: 32 (over y, x, core), space: 8 (over z).
Axes of the slice: x: 4, y: 4, z: 8, core: 2. Of those that a mesh axis runs over, the one named last changes fastest.
Arguments:
- point_states: float32 [32, 256, 1024], P('tm', 'space'), may hold values from -6 to 6
- initial_state: float32 [256, 1024], P('space'), may hold values from -6 to 6
- node_rate: float32 [256, 1024], P('space'), may hold values from 0.01 to 0.06
- source_map: float32 [256, 1024], P('space'), may hold values from -6 to 6
- waveform: float32 [512], replicated, may hold values from -2 to 2
- cond_table: float32 [16], replicated, may hold values from 0.25 to 4
- class_map: int32 [32, 8], P('space'), may hold values from 0 to 15
- interval_steps: int32 [32], replicated, may hold values from 1 to 20, 512 in all
Outputs:
- corrected: float32 [32, 256, 1024], P('tm', 'space')
The draws below stay inside these ranges and needn't reach their ends.
Inputs may be any that keep to these rules, and one draw needn't show every extreme that they name: `interval_steps`: they sum to 512 and the largest equals 20.
All inputs are finite; a program needn't handle non-finite values.
Results may differ from the reference program's by a relative error of at most 0.0003.
Values sent between devices are 32-bit elements; how exact they have to be, the bound alone decides.
A program may use at most 64 MiB of HBM per device.

```python
import math
import jax
import jax.numpy as jnp
import numpy as np
from jax import lax

NY = 1024
STEP_MOST = 20
CSUB = 5
CLASSES = 16
BLK_R = 8
BLK_C = 128
NX = 256
NCP = 32
NT = 512


def plant(result, key, low, high):
    longest = result.shape.index(max(result.shape))
    spots = []
    for shift in (0, 1):
        where = [jax.random.randint(jax.random.fold_in(key, axis), (), 0, length) for axis, length in enumerate(result.shape)]
        where[longest] = (where[longest] + shift) % result.shape[longest]
        spots.append(tuple(where))
    return result.at[spots[0]].set(low).at[spots[1]].set(high)


def block_scale(key, shape, split, least, high):
    loudness = 1.0
    for axis_at, blocks in split:
        heights = jax.random.uniform(jax.random.fold_in(jax.random.fold_in(key, 6), axis_at), (blocks,), jnp.float32, least / len(split), high / len(split))
        loudness = loudness * jnp.repeat(jnp.exp(heights), shape[axis_at] // blocks).reshape((-1,) + (1,) * (len(shape) - 1 - axis_at))
    return loudness


def profile(number_of, total, limit, lean):
    loads = [(1 << 20) // math.isqrt(rank ** lean) + 1 for rank in range(2, number_of + 1)]
    rest, given = total - limit - (number_of - 1), [1] * (number_of - 1)
    while rest > 0:
        free = [i for i in range(number_of - 1) if given[i] < limit]
        mass, remaining = sum([loads[i] for i in free]), rest
        for i in free:
            addition = min(limit - given[i], max(1, remaining * loads[i] // mass), rest)
            given[i] = given[i] + addition
            rest = rest - addition
    return np.array([limit] + given)


def uneven_parts(rng, count, total, reach, lean):
    if count == 2:
        one = jax.random.randint(rng, (), max(1, total - reach), min(reach, total - 1) + 1)
        return jnp.stack([one, total - one])
    lengths = jnp.asarray(profile(count, total, reach, lean), jnp.int32)
    twos = (count - 1) // 2
    donor, receiver = lengths[1:1 + 2 * twos:2], lengths[2:2 + 2 * twos:2]
    room = jnp.minimum(donor - 1, reach - receiver)
    moved = jax.random.randint(jax.random.fold_in(rng, 1), (twos,), 0, 1 << 20) % (room + 1)
    lengths = lengths.at[1:1 + 2 * twos:2].set(donor - moved).at[2:2 + 2 * twos:2].set(receiver + moved)
    return lengths[jax.random.permutation(jax.random.fold_in(rng, 2), count)]


def bell_draw(own_key, extent, spread, reach, cuts=(), kind=jnp.bfloat16):
    values = jax.random.normal(own_key, extent, jnp.float32) * spread
    if len(cuts) > 0:
        values = block_scale(own_key, extent, cuts, -0.22, 0.18) * values
    return jnp.clip(values, min=-reach, max=reach).astype(kind)


def setup_inputs(seed: int = 0) -> dict:
    streams_of = jax.random.split(jax.random.key(seed), 9)
    return {
        "point_states": bell_draw(streams_of[0], (NCP, NX, NY), 1.0, 6.0, ((0, 32), (1, 8)), jnp.float32),
        "initial_state": bell_draw(streams_of[1], (NX, NY), 1.0, 6.0, ((0, 8),), jnp.float32),
        "node_rate": jnp.clip(jnp.exp(math.log(0.06) - 1.7917595 * jax.random.uniform(streams_of[2], (NX, NY), jnp.float32) ** block_scale(streams_of[2], (NX, NY), ((0, 8),), -0.2, 0.2)), 0.01, 0.06),
        "source_map": bell_draw(streams_of[3], (NX, NY), 1.0, 6.0, ((0, 8),), jnp.float32),
        "waveform": bell_draw(streams_of[4], (NT,), 0.3, 2.0, (), jnp.float32),
        "cond_table": jnp.clip(jnp.exp(jax.random.uniform(streams_of[5], (CLASSES,), jnp.float32, math.log(0.25), math.log(4.0))), 0.25, 4.0),
        "class_map": plant(jax.random.randint(streams_of[6], (NX // BLK_R, NY // BLK_C), 0, CLASSES), jax.random.fold_in(streams_of[6], 1), 0, CLASSES - 1).astype(jnp.int32),
        "interval_steps": uneven_parts(streams_of[7], NCP, NT, STEP_MOST, 2).astype(jnp.int32),
    }


def neighbours(values):
    zero_row = jnp.zeros_like(values[..., :1, :])
    zero_col = jnp.zeros_like(values[..., :, :1])
    above_row = jnp.concatenate([zero_row, values[..., :-1, :]], axis=-2)
    below_row = jnp.concatenate([values[..., 1:, :], zero_row], axis=-2)
    left_col = jnp.concatenate([zero_col, values[..., :, :-1]], axis=-1)
    right_col = jnp.concatenate([values[..., :, 1:], zero_col], axis=-1)
    return (above_row, below_row, left_col, right_col)

def restrict(values):
    return 0.25 * (values[..., 0::2, 0::2] + values[..., 1::2, 0::2] + (values[..., 0::2, 1::2] + values[..., 1::2, 1::2]))

def prolong(values):
    return jnp.repeat(jnp.repeat(values, 2, axis=-2), 2, axis=-1)

def node_conductance(class_map, cond_table):
    classes = jnp.arange(cond_table.shape[0], dtype=jnp.int32)
    picked = lax.optimization_barrier(jnp.sum(jnp.where(class_map[None] == classes[:, None, None], cond_table[:, None, None], 0.0), axis=0))
    return jnp.repeat(jnp.repeat(picked, BLK_R, axis=0), BLK_C, axis=1)

def base_weights(rates, conduct):
    above_row, below_row, left_col, right_col = neighbours(conduct)
    return (rates * jnp.sqrt(conduct * above_row), rates * jnp.sqrt(conduct * below_row), rates * jnp.sqrt(conduct * left_col), rates * jnp.sqrt(conduct * right_col))

def combine(state_now, above_row, below_row, left_col, right_col, weights, forcing):
    to_above, to_below, to_left, to_right = weights
    return state_now + (to_above * (above_row - state_now) + to_below * (below_row - state_now) + to_left * (left_col - state_now) + to_right * (right_col - state_now)) + forcing

def coarse_step(carried, coarse_weights, factor):
    to_above, to_below, to_left, to_right = coarse_weights
    above_row, below_row, left_col, right_col = neighbours(carried)
    return carried + factor * (to_above * (above_row - carried) + to_below * (below_row - carried) + to_left * (left_col - carried) + to_right * (right_col - carried))

def reference(point_states, initial_state, node_rate, source_map, waveform, cond_table, class_map, interval_steps):
    conduct = node_conductance(class_map, cond_table)
    weights = base_weights(node_rate, conduct)
    coarse_weights = base_weights(restrict(node_rate), restrict(conduct))
    starts = (jnp.cumsum(interval_steps) - interval_steps).astype(jnp.int32)

    def propagate(element):
        state_in, first_step, step_count = element

        def advance(fine_step, state_now):
            above_row, below_row, left_col, right_col = neighbours(state_now)
            forcing = waveform[first_step + fine_step] * source_map
            updated = combine(state_now, above_row, below_row, left_col, right_col, weights, forcing)
            return jnp.where(fine_step < step_count, updated, state_now)
        return lax.fori_loop(0, STEP_MOST, advance, state_in)
    first_pass = lax.map(propagate, (point_states, starts, interval_steps))
    relaxed = jnp.concatenate([initial_state[None], first_pass[:-1]], axis=0)
    second_pass = lax.map(propagate, (relaxed, starts, interval_steps))
    change = restrict(second_pass - first_pass)
    coarse_res = jnp.concatenate([jnp.zeros_like(change[:1]), change[:-1]], axis=0)
    factors = interval_steps.astype(jnp.float32) / (4.0 * CSUB)

    def link(carry, link_item):
        residue, factor = link_item
        error_now = carry + residue
        carried = error_now
        for substep in range(CSUB):
            carried = coarse_step(carried, coarse_weights, factor)
        return (carried, error_now)
    unused, errors = lax.scan(link, jnp.zeros_like(coarse_res[0]), (coarse_res, factors))
    return relaxed + prolong(errors)
```

```python
import functools

import jax
import jax.numpy as jnp
from jax import lax
from jax.experimental import pallas as pl
from jax.experimental.pallas import tpu as pltpu
from jax.sharding import PartitionSpec as P

MESH = pl.DeviceIdType.MESH
STEP_MOST = 20
CSUB = 5
HALO = STEP_MOST
PAD = 24
EXT = 32 + 2 * PAD
OFF = PAD + 1
BLOCKS = EXT // 8
GROUP = 6
REACH = 2
PLAN = ((0, 3, 0, 10), (3, 11, 1, 9), (11, 19, 2, 8), (19, 20, 3, 7))


def kernel(
    dims,
    point_ref,
    init_ref,
    rate_ref,
    src_ref,
    wave_ref,
    table_ref,
    class_ref,
    steps_ref,
    out_ref,
    hist_a,
    hist_b,
    rows_rate,
    rows_src,
    weight_d,
    weight_e,
    edge,
    cond_fine,
    cond_tile,
    cond_map,
    stage,
    first,
    merge,
    split_w,
    join_w,
    own_res,
    coarse_rate,
    res_in,
    err_in,
    weight_cd,
    weight_ce,
    side_c,
    err_out,
    err_own,
    nat_rel,
    nat_err,
    s_send,
    s_halo,
    s_cond,
    s_crate,
    s_relax,
    s_res,
    s_hop,
    s_err,
):
    n_tm, n_sp, q, hs = dims
    groups = (n_tm - 2) // q
    span = 2 * hs + 1
    cext = 16 * span
    stride = cext // 8
    f32 = jnp.float32
    j = lax.axis_index("tm")
    s = lax.axis_index("space")
    pending = []

    def root_of(g):
        return (q * (g + 1) + 2) % n_tm

    def inside(t):
        return jnp.logical_and(t >= 0, t < n_sp)

    def at(cond, body):
        pl.when(cond)(body)

    group = jnp.where(j == 0, 0, (j - 1 + q) // q - 1)
    place = j - 1 - q * group
    member = jnp.logical_and(j >= 1, j <= q * groups)
    sender = j <= q * groups
    root = root_of(group)
    out_group = (j - 2 + q) // q - 1
    is_root = jnp.bool_(False)
    lead = jnp.int32(0)
    for g in range(groups):
        hit = j == root_of(g)
        is_root = jnp.logical_or(is_root, hit)
        lead = lead + jnp.where(hit, g, 0)
    reach = [d for d in range(-hs, hs + 1)]
    beside = [d for d in reach if d != 0]
    near = [-1, 0, 1]

    barrier = pltpu.get_barrier_semaphore()

    def tell(cond, tm, sp):
        def body():
            pl.semaphore_signal(barrier, inc=1, device_id=(tm, sp), device_id_type=MESH)

        at(cond, body)

    expect = jnp.int32(0)
    for d in beside:
        tell(inside(s + d), j, s + d)
        expect = expect + inside(s + d).astype(jnp.int32)
    for d in near:
        tell(jnp.logical_and(j > 0, inside(s + d)), j - 1, s + d)
        expect = expect + jnp.logical_and(j < n_tm - 1, inside(s + d)).astype(jnp.int32)
    tell(j >= 2, root_of(out_group), s)

    def greet_group():
        for d in reach:

            def body(d=d):
                for p in range(q):
                    pl.semaphore_signal(
                        barrier, inc=1, device_id=(q * lead + 1 + p, s + d), device_id_type=MESH
                    )
                pl.semaphore_signal(
                    barrier,
                    inc=1,
                    device_id=(jnp.where(lead == 0, 0, root_of(lead - 1)), s + d),
                    device_id_type=MESH,
                )

            at(inside(s + d), body)

    at(is_root, greet_group)
    strips = jnp.int32(0)
    for d in reach:
        strips = strips + inside(s + d).astype(jnp.int32)
    expect = expect + jnp.where(sender, strips, 0)
    expect = expect + jnp.where(is_root, q, 0)
    expect = expect + jnp.where(jnp.logical_and(is_root, lead < groups - 1), strips, 0)

    count = [0]

    def push(cond, src, dst, sem, tm, sp):
        slot = count[0]
        count[0] += 1

        def make():
            return pltpu.make_async_remote_copy(
                src_ref=src,
                dst_ref=dst,
                send_sem=s_send.at[slot],
                recv_sem=sem,
                device_id=(tm, sp),
                device_id_type=MESH,
            )

        at(cond, lambda: make().start())
        pending.append((cond, make))

    def arrive(cond, dst, sem):
        def body():
            pltpu.make_async_remote_copy(
                src_ref=dst,
                dst_ref=dst,
                send_sem=s_send.at[0],
                recv_sem=sem,
                device_id=(j, s),
                device_id_type=MESH,
            ).wait_recv()

        at(cond, body)

    sub = lax.broadcasted_iota(jnp.int32, (8, 128), 0)
    lane = lax.broadcasted_iota(jnp.int32, (8, 128), 1)

    def to_rows(natural, put):
        for b in range(4):
            for c in range(8):
                stage[pl.ds((b * 8 + c) * 8, 8), :] = natural[
                    pl.ds(8 * b, 8), pl.ds(128 * c, 128)
                ]
        for b in range(4):
            for i in range(8):
                put(8 * b + i, stage[pl.ds(b * 64 + i, 8, stride=8), :])

    top, bottom = s == 0, s == n_sp - 1
    up, down = s > 0, s < n_sp - 1
    zeros = jnp.zeros((PAD, 8, 128), f32)

    def put_point(r, value):
        hist_a[0, OFF + r] = value

    to_rows(point_ref.at[0], put_point)

    for i in range(4):
        fine = jnp.zeros((8, 128), f32)
        for c in range(8):
            fine = jnp.where(sub == c, table_ref[class_ref[i, c]], fine)
        cond_fine[pl.ds(32 + 8 * i, 8), :] = fine
    tile = jnp.zeros((8, 128), f32)
    for i in range(4):
        for c in range(8):
            tile = jnp.where(
                jnp.logical_and(sub == i, lane // 16 == c), table_ref[class_ref[i, c]], tile
            )
    cond_tile[hs] = tile

    def clear_top():
        hist_a[0, pl.ds(1, PAD)] = zeros
        hist_b[0, pl.ds(1, PAD)] = zeros
        rows_rate[pl.ds(0, PAD)] = zeros
        rows_src[pl.ds(0, PAD)] = zeros
        cond_fine[pl.ds(0, 32), :] = jnp.zeros((32, 128), f32)

    def clear_bottom():
        hist_a[0, pl.ds(OFF + 32, PAD)] = zeros
        hist_b[0, pl.ds(OFF + 32, PAD)] = zeros
        rows_rate[pl.ds(PAD + 32, PAD)] = zeros
        rows_src[pl.ds(PAD + 32, PAD)] = zeros
        cond_fine[pl.ds(64, 32), :] = jnp.zeros((32, 128), f32)

    at(top, clear_top)
    at(bottom, clear_bottom)

    pl.semaphore_wait(barrier, expect)

    def halos(buf, own, to_up, sems, only=None):
        a = up if only is None else jnp.logical_and(up, only)
        b = down if only is None else jnp.logical_and(down, only)
        push(a, buf.at[pl.ds(own, HALO)], buf.at[pl.ds(own + 32, HALO)], sems.at[1], j, s - 1)
        push(
            b,
            buf.at[pl.ds(own + 32 - HALO, HALO)],
            buf.at[pl.ds(own - HALO, HALO)],
            sems.at[0],
            j,
            s + 1,
        )

    def halos_in(buf, own, sems):
        arrive(up, buf.at[pl.ds(own - HALO, HALO)], sems.at[0])
        arrive(down, buf.at[pl.ds(own + 32, HALO)], sems.at[1])

    mine = cond_fine.at[pl.ds(32, 32), :]
    push(up, mine, cond_fine.at[pl.ds(64, 32), :], s_cond.at[0], j, s - 1)
    push(down, mine, cond_fine.at[pl.ds(0, 32), :], s_cond.at[1], j, s + 1)
    for d in beside:
        push(
            jnp.logical_and(is_root, inside(s + d)),
            cond_tile.at[hs],
            cond_tile.at[hs - d],
            s_crate.at[1, hs - d],
            j,
            s + d,
        )
    halos(hist_a.at[0], OFF, None, s_halo.at[0])

    def put_rate(r, value):
        rows_rate[PAD + r] = value

    def put_src(r, value):
        rows_src[PAD + r] = value

    to_rows(rate_ref, put_rate)
    halos(rows_rate, PAD, None, s_halo.at[1])
    to_rows(src_ref, put_src)
    halos(rows_src, PAD, None, s_halo.at[2])

    def place_initial():
        def put_init(r, value):
            hist_b[0, OFF + r] = value

        to_rows(init_ref, put_init)

    at(j == 0, place_initial)
    push(
        jnp.logical_and(j == 0, up),
        hist_b.at[0, pl.ds(OFF, HALO)],
        hist_b.at[0, pl.ds(OFF + 32, HALO)],
        s_relax.at[2],
        j,
        s - 1,
    )
    push(
        jnp.logical_and(j == 0, down),
        hist_b.at[0, pl.ds(OFF + 32 - HALO, HALO)],
        hist_b.at[0, pl.ds(OFF - HALO, HALO)],
        s_relax.at[0],
        j,
        s + 1,
    )

    def fill_split(i, carry):
        f = lax.broadcasted_iota(jnp.int32, (64, 512), 0) + 64 * i
        o = lax.broadcasted_iota(jnp.int32, (64, 512), 1)
        hit = jnp.logical_and((f >> 3) == (o & 127), ((f & 7) >> 1) == (o >> 7))
        split_w[pl.ds(pl.multiple_of(64 * i, 64), 64), :] = jnp.where(hit, 1.0, 0.0).astype(
            jnp.bfloat16
        )
        return carry

    def fill_join(i, carry):
        o = lax.broadcasted_iota(jnp.int32, (32, 1024), 0) + 32 * i
        f = lax.broadcasted_iota(jnp.int32, (32, 1024), 1)
        hit = jnp.logical_and((f >> 3) == (o & 127), ((f & 7) >> 1) == (o >> 7))
        join_w[pl.ds(pl.multiple_of(32 * i, 32), 32), :] = jnp.where(hit, 1.0, 0.0).astype(
            jnp.bfloat16
        )
        return carry

    lax.fori_loop(0, 16, fill_split, 0)
    lax.fori_loop(0, 16, fill_join, 0)

    def exact_dot(values, matrix):
        high = values.astype(jnp.bfloat16)
        rest = values - high.astype(f32)
        mid = rest.astype(jnp.bfloat16)
        low = (rest - mid.astype(f32)).astype(jnp.bfloat16)
        n = values.shape[0]
        parts = jnp.dot(
            jnp.concatenate([high, mid, low], axis=0), matrix, preferred_element_type=f32
        )
        return (parts[2 * n :] + parts[n : 2 * n]) + parts[:n]

    def restrict(row_pair):
        for i in range(16):
            stage[pl.ds(8 * i, 8), :] = row_pair(i)
        for b in range(2):
            for c in range(8):
                merge[pl.ds(8 * b, 8), pl.ds(128 * c, 128)] = stage[
                    pl.ds(64 * b + c, 8, stride=8), :
                ]
        return 0.25 * exact_dot(merge[...], split_w[...])

    def make_coarse_rate():
        values = restrict(lambda i: rows_rate[PAD + 2 * i] + rows_rate[PAD + 2 * i + 1])
        for m in range(4):
            coarse_rate[m, pl.ds(16 * hs, 16), :] = values[:, 128 * m : 128 * m + 128]
        for d in beside:

            def wipe(d=d):
                where = pl.ds(16 * (hs + d), 16)
                coarse_rate[:, where, :] = jnp.zeros((4, 16, 128), f32)
                err_in[:, where, :] = jnp.zeros((4, 16, 128), f32)
                for p in range(q):
                    res_in[p, :, where, :] = jnp.zeros((4, 16, 128), f32)
                cond_tile[hs + d] = jnp.zeros((8, 128), f32)

            at(jnp.logical_not(inside(s + d)), wipe)

    at(is_root, make_coarse_rate)
    for d in beside:
        push(
            jnp.logical_and(is_root, inside(s + d)),
            coarse_rate.at[:, pl.ds(16 * hs, 16), :],
            coarse_rate.at[:, pl.ds(16 * (hs - d), 16), :],
            s_crate.at[0, hs - d],
            j,
            s + d,
        )

    def add_up(i, total):
        return total + jnp.where(i < j, steps_ref[i], 0)

    start = lax.fori_loop(0, n_tm, add_up, jnp.int32(0))
    steps = steps_ref[j]

    arrive(down, cond_fine.at[pl.ds(64, 32), :], s_cond.at[0])
    arrive(up, cond_fine.at[pl.ds(0, 32), :], s_cond.at[1])
    halos_in(rows_rate, PAD, s_halo.at[1])

    for b in range(BLOCKS):
        here = cond_fine[pl.ds(8 * (b + 1), 8), :]
        safe = jnp.where(here > 0.0, here, 1.0)
        above = jnp.sqrt(cond_fine[pl.ds(8 * b, 8), :] * here) / safe
        below = jnp.sqrt(cond_fine[pl.ds(8 * (b + 2), 8), :] * here) / safe
        left = jnp.where(sub == 0, 0.0, jnp.sqrt(pltpu.roll(here, 1, 0) * here) / safe)
        right = jnp.where(sub == 7, 0.0, jnp.sqrt(pltpu.roll(here, 7, 0) * here) / safe)
        edge[b, 0] = above
        edge[b, 1] = below
        edge[b, 2] = left
        edge[b, 3] = right
        sides = jnp.where(lane == 0, left, 1.0) + jnp.where(lane == 127, right, 1.0)
        for i in range(8):
            total = sides + (above if i == 0 else 1.0) + (below if i == 7 else 1.0)
            scaled = rows_rate[8 * b + i] * here
            weight_d[8 * b + i] = scaled
            weight_e[8 * b + i] = 1.0 - scaled * total

    first_lane = lax.broadcasted_iota(jnp.int32, (8, 8, 128), 2) == 0
    last_lane = lax.broadcasted_iota(jnp.int32, (8, 8, 128), 2) == 127

    def sweep(hist):
        for n0, n1, b0, b1 in PLAN:

            def one_step(n, carry, b0=b0, b1=b1):
                amp = wave_ref[jnp.minimum(start + n, wave_ref.shape[0] - 1)]
                for b in range(b0, b1):
                    here = hist[n, pl.ds(8 * b + 1, 8)]
                    above = hist[n, pl.ds(8 * b, 8)]
                    below = hist[n, pl.ds(8 * b + 2, 8)]
                    above = jnp.concatenate([above[:1] * edge[b, 0][None], above[1:]], axis=0)
                    below = jnp.concatenate([below[:7], below[7:] * edge[b, 1][None]], axis=0)
                    left = pltpu.roll(here, 1, 2)
                    right = pltpu.roll(here, 127, 2)
                    left = jnp.where(first_lane, pltpu.roll(left, 1, 1) * edge[b, 2][None], left)
                    right = jnp.where(last_lane, pltpu.roll(right, 7, 1) * edge[b, 3][None], right)
                    hist[n + 1, pl.ds(8 * b + 1, 8)] = (
                        weight_e[pl.ds(8 * b, 8)] * here
                        + weight_d[pl.ds(8 * b, 8)] * ((above + below) + (left + right))
                        + amp * rows_src[pl.ds(8 * b, 8)]
                    )
                return carry

            lax.fori_loop(n0, n1, one_step, 0)

    halos_in(hist_a.at[0], OFF, s_halo.at[0])
    halos_in(rows_src, PAD, s_halo.at[2])
    sweep(hist_a)
    for i in range(32):
        first[i] = hist_a[steps, OFF + i]

    follow = j < n_tm - 1
    push(
        jnp.logical_and(follow, up),
        first.at[pl.ds(0, HALO)],
        hist_b.at[0, pl.ds(OFF + 32, HALO)],
        s_relax.at[2],
        j + 1,
        s - 1,
    )
    push(
        jnp.logical_and(follow, down),
        first.at[pl.ds(32 - HALO, HALO)],
        hist_b.at[0, pl.ds(OFF - HALO, HALO)],
        s_relax.at[0],
        j + 1,
        s + 1,
    )
    push(follow, first, hist_b.at[0, pl.ds(OFF, 32)], s_relax.at[1], j + 1, s)
    arrive(j > 0, hist_b.at[0, pl.ds(OFF, 32)], s_relax.at[1])
    arrive(up, hist_b.at[0, pl.ds(OFF - HALO, HALO)], s_relax.at[0])
    arrive(down, hist_b.at[0, pl.ds(OFF + 32, HALO)], s_relax.at[2])
    sweep(hist_b)

    def difference(i):
        return (hist_b[steps, OFF + 2 * i] - first[2 * i]) + (
            hist_b[steps, OFF + 2 * i + 1] - first[2 * i + 1]
        )

    change = restrict(difference)
    for m in range(4):
        own_res[m] = change[:, 128 * m : 128 * m + 128]
    wide = (q - 1 - place) * CSUB
    for d in reach:
        t_in = inside(s + d)
        for rows, low, high in ((16, 8, 1 << 20), (8, 0, 8)):
            if d == 0:
                if rows == 8:
                    continue
                cond = jnp.bool_(True)
            else:
                least = 16 * (abs(d) - 1)
                cond = jnp.logical_and(wide > least + low, wide <= least + high)
            begin = 16 - rows if d > 0 else 0
            push(
                jnp.logical_and(jnp.logical_and(member, t_in), cond),
                own_res.at[:, pl.ds(begin, rows), :],
                res_in.at[jnp.clip(place, 0, q - 1), :, pl.ds(16 * (hs - d) + begin, rows), :],
                s_res.at[jnp.clip(place, 0, q - 1), hs - d],
                root,
                s + d,
            )
        push(
            jnp.logical_and(j == 0, t_in),
            own_res,
            err_in.at[:, pl.ds(16 * (hs - d), 16), :],
            s_hop.at[hs - d],
            root,
            s + d,
        )
    push(j == 0, own_res, err_own, s_err, j + 1, s)

    leads = jnp.logical_and(is_root, jnp.bool_(True))

    def lead_setup():
        for d in reach:
            for h in range(2):
                cond_map[pl.ds(8 + 16 * (hs + d) + 8 * h, 8), :] = jnp.where(
                    sub < 4,
                    cond_tile[hs + d, pl.ds(2 * h, 1), :],
                    cond_tile[hs + d, pl.ds(2 * h + 1, 1), :],
                )
        cond_map[pl.ds(0, 8), :] = jnp.zeros((8, 128), f32)
        cond_map[pl.ds(8 + cext, 8), :] = jnp.zeros((8, 128), f32)
        factors = [steps_ref[q * lead + 1 + p].astype(f32) / (4.0 * CSUB) for p in range(q)]
        for k in range(stride):
            here = cond_map[pl.ds(8 + k, 8, stride=stride), :]
            safe = jnp.where(here > 0.0, here, 1.0)
            above = jnp.sqrt(cond_map[pl.ds(7 + k, 8, stride=stride), :] * here) / safe
            below = jnp.sqrt(cond_map[pl.ds(9 + k, 8, stride=stride), :] * here) / safe
            left = jnp.where(lane == 0, 0.0, jnp.sqrt(pltpu.roll(here, 1, 1) * here) / safe)
            right = jnp.where(lane == 127, 0.0, jnp.sqrt(pltpu.roll(here, 127, 1) * here) / safe)
            side_c[0, k] = above
            side_c[1, k] = below
            side_c[2, k] = left
            side_c[3, k] = right
            for m in range(4):
                total = (above + below) + (
                    (left if m == 0 else 1.0) + (right if m == 3 else 1.0)
                )
                scaled = coarse_rate[m, pl.ds(k, 8, stride=stride), :] * here
                for p in range(q):
                    weight_cd[p, 4 * k + m] = scaled * factors[p]
                    weight_ce[p, 4 * k + m] = 1.0 - scaled * factors[p] * total

    for d in beside:
        arrive(
            jnp.logical_and(leads, inside(s + d)),
            coarse_rate.at[:, pl.ds(16 * (hs + d), 16), :],
            s_crate.at[0, hs + d],
        )
        arrive(jnp.logical_and(leads, inside(s + d)), cond_tile.at[hs + d], s_crate.at[1, hs + d])
    at(leads, lead_setup)

    for d in reach:
        arrive(
            jnp.logical_and(leads, inside(s + d)),
            err_in.at[:, pl.ds(16 * (hs + d), 16), :],
            s_hop.at[hs + d],
        )

    def coarse_steps(p, source):
        def one(i, state):
            new = []
            for k in range(stride):
                for m in range(4):
                    v = state[4 * k + m]
                    if k > 0:
                        above = state[4 * (k - 1) + m]
                    else:
                        above = pltpu.roll(state[4 * (stride - 1) + m], 1, 0)
                    if k < stride - 1:
                        below = state[4 * (k + 1) + m]
                    else:
                        below = pltpu.roll(state[m], 7, 0)
                    if m > 0:
                        left = state[4 * k + m - 1]
                    else:
                        left = pltpu.roll(state[4 * k + 3], 1, 1) * side_c[2, k]
                    if m < 3:
                        right = state[4 * k + m + 1]
                    else:
                        right = pltpu.roll(state[4 * k], 127, 1) * side_c[3, k]
                    around = (above * side_c[0, k] + below * side_c[1, k]) + (left + right)
                    new.append(weight_ce[p, 4 * k + m] * v + weight_cd[p, 4 * k + m] * around)
            return tuple(new)

        state = tuple(
            source[m, pl.ds(k, 8, stride=stride), :]
            for k in range(stride)
            for m in range(4)
        )
        state = lax.fori_loop(0, CSUB, one, state)
        for k in range(stride):
            for m in range(4):
                where = (p, m, pl.ds(k, 8, stride=stride), slice(None))
                err_out[where] = state[4 * k + m] + res_in[where]

    for p in range(q):
        wide_p = (q - 1 - p) * CSUB
        for d in reach:
            if d != 0 and wide_p <= 16 * (abs(d) - 1):
                continue
            rows = 16 if d == 0 or wide_p > 16 * (abs(d) - 1) + 8 else 8
            begin = 16 - rows if d < 0 else 0
            arrive(
                jnp.logical_and(leads, inside(s + d)),
                res_in.at[p, :, pl.ds(16 * (hs + d) + begin, rows), :],
                s_res.at[p, hs + d],
            )
        source = err_in if p == 0 else err_out.at[p - 1]
        at(leads, functools.partial(coarse_steps, p, source))
        own = err_out.at[p, :, pl.ds(16 * hs, 16), :]
        if p == q - 1:
            for d in reach:
                push(
                    jnp.logical_and(jnp.logical_and(leads, lead < groups - 1), inside(s + d)),
                    own,
                    err_in.at[:, pl.ds(16 * (hs - d), 16), :],
                    s_hop.at[hs - d],
                    root_of(lead + 1),
                    s + d,
                )
        push(leads, own, err_own, s_err, q * lead + 2 + p, s)

    for i in range(32):
        stage[pl.ds(8 * i, 8), :] = hist_b[0, OFF + i]
    for b in range(4):
        for c in range(8):
            nat_rel[pl.ds(8 * b, 8), pl.ds(128 * c, 128)] = stage[
                pl.ds(64 * b + c, 8, stride=8), :
            ]

    def no_error():
        out_ref[0] = nat_rel[...]

    def with_error():
        errors = jnp.concatenate([err_own[m] for m in range(4)], axis=1)
        spread = exact_dot(errors, join_w[...])
        for c in range(8):
            columns = slice(128 * c, 128 * c + 128)
            nat_err[c, pl.ds(0, 16, stride=2), :] = spread[:, columns]
            nat_err[c, pl.ds(1, 16, stride=2), :] = spread[:, columns]
            out_ref[0, :, pl.ds(128 * c, 128)] = nat_rel[:, pl.ds(128 * c, 128)] + nat_err[c]

    arrive(j > 0, err_own, s_err)
    at(j == 0, no_error)
    at(j > 0, with_error)
    for cond, make in pending:
        at(cond, lambda make=make: make().wait_send())


def advance(dims, *args):
    n_tm, n_sp, q, hs = dims
    span = 2 * hs + 1
    cext = 16 * span
    planes = cext // 2
    f32 = jnp.float32
    vm = pl.BlockSpec(memory_space=pltpu.VMEM)
    sm = pl.BlockSpec(memory_space=pltpu.SMEM)
    dma = pltpu.SemaphoreType.DMA
    return pl.pallas_call(
        functools.partial(kernel, dims),
        out_shape=jax.ShapeDtypeStruct((1, 32, 1024), f32),
        in_specs=[vm] * 4 + [sm] * 4,
        out_specs=vm,
        scratch_shapes=[
            pltpu.VMEM((STEP_MOST + 1, EXT + 2, 8, 128), f32),
            pltpu.VMEM((STEP_MOST + 1, EXT + 2, 8, 128), f32),
            pltpu.VMEM((EXT, 8, 128), f32),
            pltpu.VMEM((EXT, 8, 128), f32),
            pltpu.VMEM((EXT, 8, 128), f32),
            pltpu.VMEM((EXT, 8, 128), f32),
            pltpu.VMEM((BLOCKS, 4, 8, 128), f32),
            pltpu.VMEM((96, 128), f32),
            pltpu.VMEM((span, 8, 128), f32),
            pltpu.VMEM((cext + 16, 128), f32),
            pltpu.VMEM((256, 128), f32),
            pltpu.VMEM((32, 8, 128), f32),
            pltpu.VMEM((16, 1024), f32),
            pltpu.VMEM((1024, 512), jnp.bfloat16),
            pltpu.VMEM((512, 1024), jnp.bfloat16),
            pltpu.VMEM((4, 16, 128), f32),
            pltpu.VMEM((4, cext, 128), f32),
            pltpu.VMEM((q, 4, cext, 128), f32),
            pltpu.VMEM((4, cext, 128), f32),
            pltpu.VMEM((q, planes, 8, 128), f32),
            pltpu.VMEM((q, planes, 8, 128), f32),
            pltpu.VMEM((4, cext // 8, 8, 128), f32),
            pltpu.VMEM((q, 4, cext, 128), f32),
            pltpu.VMEM((4, 16, 128), f32),
            pltpu.VMEM((32, 1024), f32),
            pltpu.VMEM((8, 32, 128), f32),
            dma((80,)),
            dma((3, 2)),
            dma((2,)),
            dma((2, span)),
            dma((3,)),
            dma((q, span)),
            dma((span,)),
            dma(()),
        ],
        compiler_params=pltpu.CompilerParams(
            collective_id=0, has_side_effects=True, vmem_limit_bytes=48 * 1024 * 1024
        ),
    )(*args)


def solution(mesh, q=GROUP, hs=REACH):
    placed = (
        P("tm", "space", None),
        P("space", None),
        P("space", None),
        P("space", None),
        P(),
        P(),
        P("space", None),
        P(),
    )
    dims = (mesh.shape["tm"], mesh.shape["space"], q, hs)
    return jax.shard_map(
        functools.partial(advance, dims),
        mesh=mesh,
        in_specs=placed,
        out_specs=P("tm", "space", None),
        check_vma=False,
    )
```

```python
import functools

import jax
import jax.numpy as jnp
from jax import lax
from jax.experimental import pallas as pl
from jax.experimental.pallas import tpu as pltpu
from jax.sharding import PartitionSpec as P

MESH = pl.DeviceIdType.MESH
STEP_MOST = 20
CSUB = 5
HALO = 24
EXT = 32 + 2 * HALO
OFF = 8
BLOCKS = EXT // 8
PLAN = ((0, 2, 0, 10), (2, 6, 1, 9), (6, 10, 2, 8))
GROUPS = (4, 13, 13)
LEADS = (6, 4, 12)


def kernel(
    dims,
    point_ref,
    init_ref,
    rate_ref,
    src_ref,
    wave_hbm,
    table_hbm,
    class_hbm,
    steps_hbm,
    out_ref,
    wave_ref,
    table_ref,
    class_ref,
    steps_ref,
    nat_point,
    nat_rate,
    nat_src,
    nat_init,
    hist_a,
    hist_b,
    hist_c,
    rows_rate,
    rows_src,
    weight_d,
    weight_e,
    edge,
    tiles,
    first,
    change,
    perm_w,
    back_w,
    join_w,
    own_res,
    coarse_rate,
    res_in,
    err_in,
    weight_cd,
    weight_ce,
    side_c,
    even,
    odd,
    even_turn,
    odd_turn,
    err_out,
    err_own,
    nat_rel,
    nat_err,
    s_local,
    s_send,
    s_errs,
    s_point,
    s_static,
    s_share,
    s_tile,
    s_crate,
    s_relax,
    s_res,
    s_hop,
    s_err,
):
    n_tm, n_sp, sizes, heads = dims
    groups = len(sizes)
    starts_of = [1 + sum(sizes[:g]) for g in range(groups + 1)]
    f32 = jnp.float32
    bf16 = jnp.bfloat16
    i32 = jnp.int32
    j = lax.axis_index("tm")
    s = lax.axis_index("space")
    twin = j + 1 - 2 * (j % 2)
    pending = []

    def at(cond, body):
        pl.when(cond)(body)

    def both(a, b):
        return jnp.logical_and(a, b)

    def pick(values, index):
        out = i32(values[0])
        for g in range(1, len(values)):
            out = jnp.where(index == g, i32(values[g]), out)
        return out

    def reach_of(rows):
        return (rows + 15) // 16

    def close(t, reach):
        return both(t - s <= reach, s - t <= reach)

    group = i32(0)
    out_group = i32(0)
    for g in range(1, groups):
        group = group + (j >= starts_of[g]).astype(i32)
        out_group = out_group + (j >= starts_of[g] + 1).astype(i32)
    sender = j < starts_of[groups]
    place = j - pick(starts_of, group)
    root = pick(heads, group)
    reach_res = jnp.where(
        j == 0, reach_of(CSUB * sizes[0]), reach_of((pick(sizes, group) - 1 - place) * CSUB)
    )
    is_root = jnp.bool_(False)
    lead = i32(0)
    for g in range(groups):
        is_root = jnp.logical_or(is_root, j == heads[g])
        lead = lead + jnp.where(j == heads[g], g, 0)
    lead_size = pick(sizes, lead)
    lead_start = pick(starts_of, lead)
    has_next = both(is_root, lead < groups - 1)
    next_lead = jnp.minimum(lead + 1, groups - 1)
    next_root = pick(heads, next_lead)
    reach_next = reach_of(CSUB * pick(sizes, next_lead))
    reach_here = reach_of(CSUB * lead_size)

    top, bottom = s == 0, s == n_sp - 1
    up, down = s > 0, s < n_sp - 1

    loads = [
        pltpu.make_async_copy(class_hbm, class_ref, s_local.at[0]),
        pltpu.make_async_copy(table_hbm, table_ref, s_local.at[1]),
        pltpu.make_async_copy(rate_ref, nat_rate.at[pl.ds(HALO, 32), :], s_local.at[2]),
        pltpu.make_async_copy(src_ref, nat_src.at[pl.ds(HALO, 32), :], s_local.at[3]),
        pltpu.make_async_copy(point_ref.at[0], nat_point.at[pl.ds(HALO, 32), :], s_local.at[4]),
        pltpu.make_async_copy(init_ref, nat_init, s_local.at[5]),
        pltpu.make_async_copy(steps_hbm, steps_ref, s_local.at[6]),
        pltpu.make_async_copy(wave_hbm, wave_ref, s_local.at[7]),
    ]
    for load in loads:
        load.start()

    barrier = pltpu.get_barrier_semaphore()
    expect = i32(1)

    def signal(tm, sp):
        pl.semaphore_signal(barrier, inc=1, device_id=(tm, sp), device_id_type=MESH)

    def tell(cond, tm, sp):
        at(cond, lambda: signal(tm, sp))

    signal(twin, s)
    for t in range(n_sp):
        beside = both(t != s, jnp.logical_or(is_root, close(t, 1)))
        tell(beside, j, t)
        tell(both(j > 0, close(t, 1)), j - 1, t)
        expect = expect + beside.astype(i32)
        expect = expect + both(j < n_tm - 1, close(t, 1)).astype(i32)
        expect = expect + both(sender, close(t, reach_res)).astype(i32)
        expect = expect + both(has_next, close(t, reach_next)).astype(i32)
    tell(j >= 2, pick(heads, out_group), s)
    expect = expect + jnp.where(is_root, lead_size, 0)

    def greet_group():
        before = jnp.where(lead == 0, 0, pick(heads, jnp.maximum(lead - 1, 0)))
        for t in range(n_sp):
            tell(close(t, reach_here), before, t)

        def one(p, carry):
            reach = reach_of((lead_size - 1 - p) * CSUB)
            for t in range(n_sp):
                tell(close(t, reach), lead_start + p, t)
            return carry

        lax.fori_loop(0, lead_size, one, 0)

    at(is_root, greet_group)

    count = [0]

    def push(cond, src, dst, sem, tm, sp):
        slot = count[0]
        count[0] += 1

        def make():
            return pltpu.make_async_remote_copy(
                src_ref=src,
                dst_ref=dst,
                send_sem=s_send.at[slot],
                recv_sem=sem,
                device_id=(tm, sp),
                device_id_type=MESH,
            )

        at(cond, lambda: make().start())
        pending.append((cond, make))

    def arrive(cond, dst, sem):
        def body():
            pltpu.make_async_remote_copy(
                src_ref=dst,
                dst_ref=dst,
                send_sem=s_send.at[0],
                recv_sem=sem,
                device_id=(j, s),
                device_id_type=MESH,
            ).wait_recv()

        at(cond, body)

    sub = lax.broadcasted_iota(i32, (8, 128), 0)
    lane = lax.broadcasted_iota(i32, (8, 128), 1)
    above_rows, own_rows, below_rows = pl.ds(0, HALO), pl.ds(HALO, 32), pl.ds(HALO + 32, HALO)
    h_above, h_own, h_below = pl.ds(OFF, HALO), pl.ds(OFF + HALO, 32), pl.ds(OFF + HALO + 32, HALO)

    def clear(where, h_where, tile):
        for buf in (nat_point, nat_rate, nat_src):
            buf[where, :] = jnp.zeros((HALO, 1024), f32)
        hist_c[0, :, h_where, :] = jnp.zeros((8, HALO, 128), f32)
        tiles[pl.ds(8 * tile, 8), :] = jnp.zeros((8, 128), f32)

    at(top, lambda: clear(above_rows, h_above, 0))
    at(bottom, lambda: clear(below_rows, h_below, n_sp + 1))

    loads[0].wait()
    loads[1].wait()
    tile = jnp.zeros((8, 128), f32)
    for i in range(4):
        for c in range(8):
            tile = jnp.where(both(sub == i, lane // 16 == c), table_ref[class_ref[i, c]], tile)
    my_tile = tiles.at[pl.ds(pl.multiple_of(8 * s + 8, 8), 8), :]
    my_tile[...] = tile

    def fill_perm(i, carry):
        f = lax.broadcasted_iota(i32, (64, 1024), 0) + 64 * i
        o = lax.broadcasted_iota(i32, (64, 1024), 1)
        hit = o == ((f & 7) << 7) + (f >> 3)
        perm_w[pl.ds(pl.multiple_of(64 * i, 64), 64), :] = jnp.where(hit, 1.0, 0.0).astype(bf16)
        return carry

    lax.fori_loop(0, 16, fill_perm, 0)

    pl.semaphore_wait(barrier, expect)

    for t in range(n_sp):
        push(
            both(t != s, jnp.logical_or(is_root, close(t, 1))), my_tile, my_tile, s_tile.at[s], j, t
        )
    low, high = pl.ds(0, HALO), pl.ds(32 - HALO, HALO)
    first_core, second_core = j % 2 == 0, j % 2 == 1
    for core, ref, nat in ((first_core, rate_ref, nat_rate), (second_core, src_ref, nat_src)):
        push(both(core, up), ref.at[low, :], nat.at[below_rows, :], s_static.at[1], j, s - 1)
        push(both(core, down), ref.at[high, :], nat.at[above_rows, :], s_static.at[0], j, s + 1)
    push(up, point_ref.at[0, low, :], nat_point.at[below_rows, :], s_point.at[1], j, s - 1)
    push(down, point_ref.at[0, high, :], nat_point.at[above_rows, :], s_point.at[0], j, s + 1)

    def exact_dot(values, matrix):
        large = values.astype(bf16)
        rest = values - large.astype(f32)
        mid = rest.astype(bf16)
        small = (rest - mid.astype(f32)).astype(bf16)
        n = values.shape[0]
        parts = jnp.dot(
            jnp.concatenate([large, mid, small], axis=0), matrix[...], preferred_element_type=f32
        )
        return (parts[2 * n :] + parts[n : 2 * n]) + parts[:n]

    def to_parts(nat, put):
        moved = exact_dot(nat[own_rows, :], perm_w)
        for m in range(8):
            put(m, 0, moved[:, 128 * m : 128 * m + 128])

    def halos_to_parts(nat, put):
        moved = exact_dot(jnp.concatenate([nat[above_rows, :], nat[below_rows, :]], axis=0), perm_w)
        for m in range(8):
            columns = slice(128 * m, 128 * m + 128)
            put(m, -1, moved[:HALO, columns])
            put(m, 1, moved[HALO:, columns])

    rows_at = {-1: above_rows, 0: own_rows, 1: below_rows}
    h_rows_at = {-1: h_above, 0: h_own, 1: h_below}

    def put_in(ref):
        def put(m, which, value):
            ref[m, rows_at[which], :] = value

        return put

    def put_point(m, which, value):
        hist_a[0, m, h_rows_at[which], :] = value

    loads[2].wait()
    to_parts(nat_rate, put_in(rows_rate))

    mine16 = pl.ds(pl.multiple_of(16 * s, 16), 16)

    def make_coarse_rate():
        for m in range(4):
            parts = []
            for side in (0, 1):
                part = rows_rate.at[2 * m + side]
                a = part[pl.ds(HALO, 16, stride=2), :]
                parts.append(a + part[pl.ds(HALO + 1, 16, stride=2), :])
            coarse_rate[m, mine16, :] = 0.25 * (parts[0] + parts[1])

    at(is_root, make_coarse_rate)
    for t in range(n_sp):
        strip = coarse_rate.at[:, mine16, :]
        push(both(is_root, t != s), strip, strip, s_crate.at[s], j, t)

    loads[3].wait()
    to_parts(nat_src, put_in(rows_src))
    loads[4].wait()
    to_parts(nat_point, put_point)
    loads[5].wait()

    def place_initial():
        moved = exact_dot(nat_init[...], perm_w)
        for m in range(8):
            hist_c[0, m, h_own, :] = moved[:, 128 * m : 128 * m + 128]

    at(j == 0, place_initial)
    at_c = hist_c.at[0]
    push(
        both(j == 0, up),
        at_c.at[:, pl.ds(OFF + HALO, HALO), :],
        at_c.at[:, h_below, :],
        s_relax.at[2],
        j,
        s - 1,
    )
    push(
        both(j == 0, down),
        at_c.at[:, pl.ds(OFF + 32, HALO), :],
        at_c.at[:, h_above, :],
        s_relax.at[0],
        j,
        s + 1,
    )

    def fill_back(i, carry):
        o = lax.broadcasted_iota(i32, (64, 1024), 0) + 64 * i
        f = lax.broadcasted_iota(i32, (64, 1024), 1)
        hit = f == ((o & 127) << 3) + (o >> 7)
        back_w[pl.ds(pl.multiple_of(64 * i, 64), 64), :] = jnp.where(hit, 1.0, 0.0).astype(bf16)
        return carry

    def fill_join(i, carry):
        o = lax.broadcasted_iota(i32, (64, 1024), 0) + 64 * i
        f = lax.broadcasted_iota(i32, (64, 1024), 1)
        hit = (f >> 1) == ((o & 127) << 2) + (o >> 7)
        join_w[pl.ds(pl.multiple_of(64 * i, 64), 64), :] = jnp.where(hit, 1.0, 0.0).astype(bf16)
        return carry

    lax.fori_loop(0, 16, fill_back, 0)
    lax.fori_loop(0, 8, fill_join, 0)

    loads[6].wait()
    loads[7].wait()

    def add_up(i, total):
        return total + jnp.where(i < j, steps_ref[i], 0)

    start = lax.fori_loop(0, n_tm, add_up, i32(0))
    steps = steps_ref[j]

    for core, nat, other in ((first_core, nat_rate, nat_src), (second_core, nat_src, nat_rate)):
        for side, where, sem in ((up, above_rows, 0), (down, below_rows, 1)):
            cond = both(core, side)
            arrive(cond, nat.at[where, :], s_static.at[sem])
            push(cond, nat.at[where, :], nat.at[where, :], s_share.at[sem], twin, s)
    for t in range(n_sp):
        arrive(both(t != s, close(t, 1)), tiles.at[pl.ds(8 * t + 8, 8), :], s_tile.at[t])

    def block_row(b):
        strip, row = (b + 1) // 4, (b + 1) % 4
        line = tiles[pl.ds(pl.multiple_of(8 * s + 8 * strip, 8), 8), :][row : row + 1, :]
        return jnp.broadcast_to(line, (8, 128))

    for b in range(BLOCKS):
        here = block_row(b)
        safe = jnp.where(here > 0.0, here, 1.0)
        edge[b, 0] = jnp.where(sub == 0, jnp.sqrt(block_row(b - 1) * here) / safe, 1.0)
        edge[b, 1] = jnp.where(sub == 7, jnp.sqrt(block_row(b + 1) * here) / safe, 1.0)
        edge[b, 2] = jnp.where(lane == 0, 0.0, jnp.sqrt(pltpu.roll(here, 1, 1) * here) / safe)
        edge[b, 3] = jnp.where(lane == 127, 0.0, jnp.sqrt(pltpu.roll(here, 127, 1) * here) / safe)
        edge[b, 4] = here

    def weigh(blocks):
        for b in blocks:
            rows = pl.ds(8 * b, 8)
            here = edge[b, 4]
            ends = edge[b, 0] + edge[b, 1]
            for m in range(8):
                total = ends + (
                    (edge[b, 2] if m == 0 else 1.0) + (edge[b, 3] if m == 7 else 1.0)
                )
                scaled = rows_rate[m, rows, :] * here
                weight_d[m, rows, :] = scaled
                weight_e[m, rows, :] = 1.0 - scaled * total

    weigh(range(3, 7))
    for core, nat in ((first_core, nat_src), (second_core, nat_rate)):
        for side, where, sem in ((up, above_rows, 0), (down, below_rows, 1)):
            arrive(both(core, side), nat.at[where, :], s_share.at[sem])
    halos_to_parts(nat_rate, put_in(rows_rate))
    halos_to_parts(nat_src, put_in(rows_src))
    weigh((0, 1, 2, 7, 8, 9))
    arrive(up, nat_point.at[above_rows, :], s_point.at[0])
    arrive(down, nat_point.at[below_rows, :], s_point.at[1])
    halos_to_parts(nat_point, put_point)

    def half(read, write, amp, b0, b1):
        for b in range(b0, b1):
            r0 = OFF + 8 * b
            rows = pl.ds(8 * b, 8)
            cur = [read[m, pl.ds(r0, 8), :] for m in range(8)]
            far_left = pltpu.roll(cur[7], 1, 1) * edge[b, 2]
            far_right = pltpu.roll(cur[0], 127, 1) * edge[b, 3]
            for m in (1, 2, 3, 4, 5, 6, 0, 7):
                left = cur[m - 1] if m > 0 else far_left
                right = cur[m + 1] if m < 7 else far_right
                above = read[m, pl.ds(r0 - 1, 8), :] * edge[b, 0]
                below = read[m, pl.ds(r0 + 1, 8), :] * edge[b, 1]
                write[m, pl.ds(r0, 8), :] = (
                    weight_e[m, rows, :] * cur[m]
                    + weight_d[m, rows, :] * ((above + below) + (left + right))
                    + amp * rows_src[m, rows, :]
                )

    def sweep(hist):
        last = wave_ref.shape[0] - 1
        for k0, k1, b0, b1 in PLAN:

            def two_steps(k, carry, b0=b0, b1=b1):
                half(hist.at[k], hist_b.at[k], wave_ref[jnp.minimum(start + 2 * k, last)], b0, b1)
                half(
                    hist_b.at[k],
                    hist.at[k + 1],
                    wave_ref[jnp.minimum(start + 2 * k + 1, last)],
                    b0,
                    b1,
                )
                return carry

            lax.fori_loop(k0, k1, two_steps, 0)

    pair = steps >> 1
    odd_count = (steps & 1) == 1

    def state_after(hist, m, where):
        return jnp.where(odd_count, hist_b[pair, m, where, :], hist[pair, m, where, :])

    sweep(hist_a)
    for m in range(8):
        first[m] = state_after(hist_a, m, h_own)

    follow = j < n_tm - 1
    push(
        both(follow, up), first.at[:, low, :], at_c.at[:, h_below, :], s_relax.at[2], j + 1, s - 1
    )
    push(
        both(follow, down), first.at[:, high, :], at_c.at[:, h_above, :], s_relax.at[0], j + 1, s + 1
    )
    push(follow, first, at_c.at[:, h_own, :], s_relax.at[1], j + 1, s)
    arrive(j > 0, at_c.at[:, h_own, :], s_relax.at[1])
    arrive(up, at_c.at[:, h_above, :], s_relax.at[0])
    arrive(down, at_c.at[:, h_below, :], s_relax.at[2])
    sweep(hist_c)

    for m in range(8):
        change[m] = state_after(hist_c, m, h_own) - first[m]
    for m in range(4):
        parts = []
        for side in (0, 1):
            part = change.at[2 * m + side]
            parts.append(part[pl.ds(0, 16, stride=2), :] + part[pl.ds(1, 16, stride=2), :])
        own_res[m] = 0.25 * (parts[0] + parts[1])
    slot = jnp.clip(place, 0, max(sizes) - 1)
    for t in range(n_sp):
        cond = both(sender, close(t, reach_res))
        push(both(cond, j > 0), own_res, res_in.at[slot, :, mine16, :], s_res.at[slot, s], root, t)
        push(both(cond, j == 0), own_res, err_in.at[:, mine16, :], s_hop.at[s], root, t)
    push(j == 0, own_res, err_own, s_err, j + 1, s)

    def lead_setup():
        block = [tiles[pl.ds(8 + i, n_sp, stride=8), :] for i in range(4)]
        if n_sp < 8:
            rest = jnp.zeros((8 - n_sp, 128), f32)
            block = [jnp.concatenate([v, rest], axis=0) for v in block]
        for i in range(4):
            here = block[i]
            safe = jnp.where(here > 0.0, here, 1.0)
            above = block[i - 1] if i > 0 else jnp.where(sub == 0, 0.0, pltpu.roll(block[3], 1, 0))
            below = block[i + 1] if i < 3 else jnp.where(sub == 7, 0.0, pltpu.roll(block[0], 7, 0))
            side_c[0, i] = jnp.sqrt(above * here) / safe
            side_c[1, i] = jnp.sqrt(below * here) / safe
            side_c[2, i] = jnp.where(lane == 0, 0.0, jnp.sqrt(pltpu.roll(here, 1, 1) * here) / safe)
            side_c[3, i] = jnp.where(
                lane == 127, 0.0, jnp.sqrt(pltpu.roll(here, 127, 1) * here) / safe
            )
            for k in range(4 * i, 4 * i + 4):
                for m in range(4):
                    total = (
                        (side_c[0, i] if k % 4 == 0 else 1.0)
                        + (side_c[1, i] if k % 4 == 3 else 1.0)
                    ) + (
                        (side_c[2, i] if m == 0 else 1.0) + (side_c[3, i] if m == 3 else 1.0)
                    )
                    scaled = coarse_rate[m, pl.ds(k, 8, stride=16), :] * here
                    even[4 * k + m] = scaled
                    odd[4 * k + m] = scaled * total

        def one(p, carry):
            factor = steps_ref[lead_start + p].astype(f32) * (1.0 / (4.0 * CSUB))
            for v in range(64):
                weight_cd[p, v] = even[v] * factor
                weight_ce[p, v] = 1.0 - odd[v] * factor
            return carry

        lax.fori_loop(0, lead_size, one, 0)

    for t in range(n_sp):
        far = both(is_root, t != s)
        arrive(far, coarse_rate.at[:, pl.ds(16 * t, 16), :], s_crate.at[t])
        arrive(
            both(far, jnp.logical_not(close(t, 1))),
            tiles.at[pl.ds(8 * t + 8, 8), :],
            s_tile.at[t],
        )
    at(is_root, lead_setup)
    for t in range(n_sp):
        arrive(
            both(is_root, close(t, reach_here)), err_in.at[:, pl.ds(16 * t, 16), :], s_hop.at[t]
        )

    order = [k for k in range(2, 16, 2)] + [0] + [k for k in range(1, 16, 2)]

    def coarse_step(p, read, write, turned, turns, last):
        wrap_top = [jnp.where(sub == 0, 0.0, pltpu.roll(read[60 + m], 1, 0)) for m in range(4)]
        wrap_bottom = [jnp.where(sub == 7, 0.0, pltpu.roll(read[m], 7, 0)) for m in range(4)]
        for k in order:
            i = k // 4
            for m in (0, 3, 1, 2):
                v = 4 * k + m
                above = read[v - 4] if k > 0 else wrap_top[m]
                below = read[v + 4] if k < 15 else wrap_bottom[m]
                left = read[v - 1] if m > 0 else turned[0, k] * side_c[2, i]
                right = read[v + 1] if m < 3 else turned[1, k] * side_c[3, i]
                if k % 4 == 0:
                    above = above * side_c[0, i]
                if k % 4 == 3:
                    below = below * side_c[1, i]
                new = weight_ce[p, v] * read[v] + weight_cd[p, v] * (
                    (above + below) + (left + right)
                )
                if last:
                    where = (p, m, pl.ds(k, 8, stride=16), slice(None))
                    new = new + res_in[where]
                    err_out[where] = new
                write[v] = new
                if m == 3:
                    turns[0, k] = pltpu.roll(new, 1, 1)
                if m == 0:
                    turns[1, k] = pltpu.roll(new, 127, 1)

    def err_copy(p):
        return pltpu.make_async_remote_copy(
            src_ref=err_out.at[p, :, mine16, :],
            dst_ref=err_own,
            send_sem=s_errs.at[p],
            recv_sem=s_err,
            device_id=(lead_start + 1 + p, s),
            device_id_type=MESH,
        )

    def chain():
        for k in range(16):
            for m in range(4):
                even[4 * k + m] = err_in[m, pl.ds(k, 8, stride=16), :]
            even_turn[0, k] = pltpu.roll(even[4 * k + 3], 1, 1)
            even_turn[1, k] = pltpu.roll(even[4 * k], 127, 1)

        def stage(p, carry):
            reach = reach_of((lead_size - 1 - p) * CSUB)
            for t in range(n_sp):
                arrive(close(t, reach), res_in.at[p, :, pl.ds(16 * t, 16), :], s_res.at[p, t])
            for i in range(CSUB):
                if i % 2 == 0:
                    coarse_step(p, even, odd, even_turn, odd_turn, i == CSUB - 1)
                else:
                    coarse_step(p, odd, even, odd_turn, even_turn, False)
            at(p < lead_size - 1, lambda: err_copy(p).start())
            for v in range(64):
                even[v] = odd[v]
            for k in range(16):
                even_turn[0, k] = odd_turn[0, k]
                even_turn[1, k] = odd_turn[1, k]
            return carry

        lax.fori_loop(0, lead_size, stage, 0)

    at(is_root, chain)
    end = jnp.maximum(lead_size - 1, 0)
    for t in sorted(range(n_sp), key=lambda t: -abs(2 * t - n_sp + 1)):
        push(
            both(has_next, close(t, reach_next)),
            err_out.at[end, :, mine16, :],
            err_in.at[:, mine16, :],
            s_hop.at[s],
            next_root,
            t,
        )
    at(is_root, lambda: err_copy(end).start())

    relaxed = jnp.concatenate([hist_c[0, m, h_own, :] for m in range(8)], axis=1)
    nat_rel[...] = exact_dot(relaxed, back_w)

    def no_error():
        out_ref[0] = nat_rel[...]

    def with_error():
        errors = jnp.concatenate([err_own[m] for m in range(4)], axis=1)
        spread = exact_dot(errors, join_w)
        for c in range(8):
            columns = slice(128 * c, 128 * c + 128)
            nat_err[c, pl.ds(0, 16, stride=2), :] = spread[:, columns]
            nat_err[c, pl.ds(1, 16, stride=2), :] = spread[:, columns]
            out_ref[0, :, pl.ds(128 * c, 128)] = nat_rel[:, pl.ds(128 * c, 128)] + nat_err[c]

    arrive(j > 0, err_own, s_err)
    at(j == 0, no_error)
    at(j > 0, with_error)
    for cond, make in pending:
        at(cond, lambda make=make: make().wait_send())

    def drain():
        def one(p, carry):
            err_copy(p).wait_send()
            return carry

        lax.fori_loop(0, lead_size, one, 0)

    at(is_root, drain)


def advance(dims, *args):
    n_tm, n_sp, sizes, heads = dims
    most = max(sizes)
    f32 = jnp.float32
    bf16 = jnp.bfloat16
    vm = pltpu.VMEM
    sm = pltpu.SMEM
    dma = pltpu.SemaphoreType.DMA
    hist = (STEP_MOST // 2 + 1, 8, EXT + 2 * OFF, 128)
    hbm = pl.BlockSpec(memory_space=pltpu.HBM)
    return pl.pallas_call(
        functools.partial(kernel, dims),
        out_shape=jax.ShapeDtypeStruct((1, 32, 1024), f32),
        in_specs=[hbm] * 8,
        out_specs=pl.BlockSpec(memory_space=pltpu.VMEM),
        scratch_shapes=[
            sm(args[4].shape, f32),
            sm(args[5].shape, f32),
            sm(args[6].shape, jnp.int32),
            sm(args[7].shape, jnp.int32),
            vm((EXT, 1024), f32),
            vm((EXT, 1024), f32),
            vm((EXT, 1024), f32),
            vm((32, 1024), f32),
            vm(hist, f32),
            vm(hist, f32),
            vm(hist, f32),
            vm((8, EXT, 128), f32),
            vm((8, EXT, 128), f32),
            vm((8, EXT, 128), f32),
            vm((8, EXT, 128), f32),
            vm((BLOCKS, 5, 8, 128), f32),
            vm((8 * (n_sp + 2), 128), f32),
            vm((8, 32, 128), f32),
            vm((8, 32, 128), f32),
            vm((1024, 1024), bf16),
            vm((1024, 1024), bf16),
            vm((512, 1024), bf16),
            vm((4, 16, 128), f32),
            vm((4, 128, 128), f32),
            vm((most, 4, 128, 128), f32),
            vm((4, 128, 128), f32),
            vm((most, 64, 8, 128), f32),
            vm((most, 64, 8, 128), f32),
            vm((4, 4, 8, 128), f32),
            vm((64, 8, 128), f32),
            vm((64, 8, 128), f32),
            vm((2, 16, 8, 128), f32),
            vm((2, 16, 8, 128), f32),
            vm((most, 4, 128, 128), f32),
            vm((4, 16, 128), f32),
            vm((32, 1024), f32),
            vm((8, 32, 128), f32),
            dma((8,)),
            dma((72,)),
            dma((most,)),
            dma((2,)),
            dma((2,)),
            dma((2,)),
            dma((8,)),
            dma((8,)),
            dma((3,)),
            dma((most, 8)),
            dma((8,)),
            dma(()),
        ],
        compiler_params=pltpu.CompilerParams(
            collective_id=0, has_side_effects=True, vmem_limit_bytes=66846720
        ),
    )(*args)


def solution(mesh, sizes=GROUPS, heads=LEADS):
    placed = (
        P("tm", "space", None),
        P("space", None),
        P("space", None),
        P("space", None),
        P(),
        P(),
        P("space", None),
        P(),
    )
    dims = (mesh.shape["tm"], mesh.shape["space"], sizes, heads)
    return jax.shard_map(
        functools.partial(advance, dims),
        mesh=mesh,
        in_specs=placed,
        out_specs=P("tm", "space", None),
        check_vma=False,
    )
```

```python
import functools

import jax
import jax.numpy as jnp
from jax import lax
from jax.experimental import pallas as pl
from jax.experimental.pallas import tpu as pltpu
from jax.sharding import PartitionSpec as P

MESH = pl.DeviceIdType.MESH
STEP_MOST = 20
CSUB = 5
HALO = 24
EXT = 32 + 2 * HALO
OFF = 8
BLOCKS = EXT // 8
PLAN = ((0, 2, 0, 10), (2, 6, 1, 9), (6, 10, 2, 8))
GROUPS = (4, 12, 14)
LEADS = (6, 4, 12)


def kernel(
    dims,
    point_ref,
    init_ref,
    rate_ref,
    src_ref,
    wave_hbm,
    table_hbm,
    class_hbm,
    steps_hbm,
    out_ref,
    wave_ref,
    table_ref,
    class_ref,
    steps_ref,
    nat_point,
    nat_rate,
    nat_src,
    nat_init,
    hist_a,
    hist_b,
    hist_c,
    rows_rate,
    rows_src,
    weight_d,
    weight_e,
    edge,
    tiles,
    first,
    change,
    perm_w,
    back_w,
    join_w,
    own_res,
    coarse_rate,
    res_in,
    err_in,
    weight_cd,
    weight_ce,
    side_c,
    even,
    odd,
    even_turn,
    odd_turn,
    err_out,
    err_own,
    nat_rel,
    nat_err,
    s_ready,
    s_local,
    s_send,
    s_errs,
    s_point,
    s_static,
    s_share,
    s_tile,
    s_crate,
    s_relax,
    s_res,
    s_hop,
    s_err,
):
    n_tm, n_sp, sizes, heads = dims
    groups = len(sizes)
    starts_of = [1 + sum(sizes[:g]) for g in range(groups + 1)]
    f32 = jnp.float32
    bf16 = jnp.bfloat16
    i32 = jnp.int32
    j = lax.axis_index("tm")
    s = lax.axis_index("space")
    twin = j + 1 - 2 * (j % 2)
    pending = []

    def at(cond, body):
        pl.when(cond)(body)

    def both(a, b):
        return jnp.logical_and(a, b)

    def pick(values, index):
        out = i32(values[0])
        for g in range(1, len(values)):
            out = jnp.where(index == g, i32(values[g]), out)
        return out

    def reach_of(rows):
        return (rows + 15) // 16

    def close(t, reach):
        return both(t - s <= reach, s - t <= reach)

    group = i32(0)
    out_group = i32(0)
    for g in range(1, groups):
        group = group + (j >= starts_of[g]).astype(i32)
        out_group = out_group + (j >= starts_of[g] + 1).astype(i32)
    sender = j < starts_of[groups]
    place = j - pick(starts_of, group)
    root = pick(heads, group)
    reach_res = jnp.where(
        j == 0, reach_of(CSUB * sizes[0]), reach_of((pick(sizes, group) - 1 - place) * CSUB)
    )
    is_root = jnp.bool_(False)
    lead = i32(0)
    for g in range(groups):
        is_root = jnp.logical_or(is_root, j == heads[g])
        lead = lead + jnp.where(j == heads[g], g, 0)
    lead_size = pick(sizes, lead)
    lead_start = pick(starts_of, lead)
    has_next = both(is_root, lead < groups - 1)
    next_lead = jnp.minimum(lead + 1, groups - 1)
    next_root = pick(heads, next_lead)
    reach_next = reach_of(CSUB * pick(sizes, next_lead))
    reach_here = reach_of(CSUB * lead_size)

    top, bottom = s == 0, s == n_sp - 1
    up, down = s > 0, s < n_sp - 1

    loads = [
        pltpu.make_async_copy(class_hbm, class_ref, s_local.at[0]),
        pltpu.make_async_copy(table_hbm, table_ref, s_local.at[1]),
        pltpu.make_async_copy(rate_ref, nat_rate.at[pl.ds(HALO, 32), :], s_local.at[2]),
        pltpu.make_async_copy(src_ref, nat_src.at[pl.ds(HALO, 32), :], s_local.at[3]),
        pltpu.make_async_copy(point_ref.at[0], nat_point.at[pl.ds(HALO, 32), :], s_local.at[4]),
        pltpu.make_async_copy(init_ref, nat_init, s_local.at[5]),
        pltpu.make_async_copy(steps_hbm, steps_ref, s_local.at[6]),
        pltpu.make_async_copy(wave_hbm, wave_ref, s_local.at[7]),
    ]
    for load in loads:
        load.start()

    barrier = pltpu.get_barrier_semaphore()
    expect = i32(1)

    def signal(tm, sp):
        pl.semaphore_signal(barrier, inc=1, device_id=(tm, sp), device_id_type=MESH)

    def tell(cond, tm, sp):
        at(cond, lambda: signal(tm, sp))

    tell(sender, root, s)
    tell(j >= 2, pick(heads, out_group), s)
    tell(has_next, next_root, s)
    signal(twin, s)
    for t in range(n_sp):
        beside = both(t != s, jnp.logical_or(is_root, close(t, 1)))
        tell(beside, j, t)
        tell(both(j > 0, close(t, 1)), j - 1, t)
        expect = expect + beside.astype(i32)
        expect = expect + both(j < n_tm - 1, close(t, 1)).astype(i32)
    expect = expect + jnp.where(is_root, 2 * lead_size + 1, 0)

    count = [0]

    def push(cond, src, dst, sem, tm, sp):
        slot = count[0]
        count[0] += 1

        def make():
            return pltpu.make_async_remote_copy(
                src_ref=src,
                dst_ref=dst,
                send_sem=s_send.at[slot],
                recv_sem=sem,
                device_id=(tm, sp),
                device_id_type=MESH,
            )

        at(cond, lambda: make().start())
        pending.append((cond, make))

    def arrive(cond, dst, sem):
        def body():
            pltpu.make_async_remote_copy(
                src_ref=dst,
                dst_ref=dst,
                send_sem=s_send.at[0],
                recv_sem=sem,
                device_id=(j, s),
                device_id_type=MESH,
            ).wait_recv()

        at(cond, body)

    sub = lax.broadcasted_iota(i32, (8, 128), 0)
    lane = lax.broadcasted_iota(i32, (8, 128), 1)
    above_rows, own_rows, below_rows = pl.ds(0, HALO), pl.ds(HALO, 32), pl.ds(HALO + 32, HALO)
    h_above, h_own, h_below = pl.ds(OFF, HALO), pl.ds(OFF + HALO, 32), pl.ds(OFF + HALO + 32, HALO)

    def clear(where, h_where, tile):
        for buf in (nat_point, nat_rate, nat_src):
            buf[where, :] = jnp.zeros((HALO, 1024), f32)
        hist_c[0, :, h_where, :] = jnp.zeros((8, HALO, 128), f32)
        tiles[pl.ds(8 * tile, 8), :] = jnp.zeros((8, 128), f32)

    at(top, lambda: clear(above_rows, h_above, 0))
    at(bottom, lambda: clear(below_rows, h_below, n_sp + 1))

    loads[0].wait()
    loads[1].wait()
    tile = jnp.zeros((8, 128), f32)
    for i in range(4):
        for c in range(8):
            tile = jnp.where(both(sub == i, lane // 16 == c), table_ref[class_ref[i, c]], tile)
    my_tile = tiles.at[pl.ds(pl.multiple_of(8 * s + 8, 8), 8), :]
    my_tile[...] = tile

    def fill_perm(i, carry):
        f = lax.broadcasted_iota(i32, (64, 1024), 0) + 64 * i
        o = lax.broadcasted_iota(i32, (64, 1024), 1)
        hit = o == ((f & 7) << 7) + (f >> 3)
        perm_w[pl.ds(pl.multiple_of(64 * i, 64), 64), :] = jnp.where(hit, 1.0, 0.0).astype(bf16)
        return carry

    lax.fori_loop(0, 16, fill_perm, 0)

    pl.semaphore_wait(barrier, expect)

    for t in range(n_sp):
        push(
            both(t != s, jnp.logical_or(is_root, close(t, 1))), my_tile, my_tile, s_tile.at[s], j, t
        )
    low, high = pl.ds(0, HALO), pl.ds(32 - HALO, HALO)
    first_core, second_core = j % 2 == 0, j % 2 == 1
    for core, ref, nat in ((first_core, rate_ref, nat_rate), (second_core, src_ref, nat_src)):
        push(both(core, up), ref.at[low, :], nat.at[below_rows, :], s_static.at[1], j, s - 1)
        push(both(core, down), ref.at[high, :], nat.at[above_rows, :], s_static.at[0], j, s + 1)
    push(up, point_ref.at[0, low, :], nat_point.at[below_rows, :], s_point.at[1], j, s - 1)
    push(down, point_ref.at[0, high, :], nat_point.at[above_rows, :], s_point.at[0], j, s + 1)

    def answer():
        def ready(which, tm):
            pl.semaphore_signal(
                s_ready.at[which], inc=1, device_id=(tm, s), device_id_type=MESH
            )

        def one(p, carry):
            ready(0, lead_start + p)
            return carry

        lax.fori_loop(0, lead_size, one, 0)
        at(lead == 0, lambda: ready(0, 0))
        at(lead > 0, lambda: ready(1, pick(heads, jnp.maximum(lead - 1, 0))))

    at(is_root, answer)

    def exact_dot(values, matrix):
        large = values.astype(bf16)
        rest = values - large.astype(f32)
        mid = rest.astype(bf16)
        small = (rest - mid.astype(f32)).astype(bf16)
        n = values.shape[0]
        parts = jnp.dot(
            jnp.concatenate([large, mid, small], axis=0), matrix[...], preferred_element_type=f32
        )
        return (parts[2 * n :] + parts[n : 2 * n]) + parts[:n]

    def to_parts(nat, put):
        moved = exact_dot(nat[own_rows, :], perm_w)
        for m in range(8):
            put(m, 0, moved[:, 128 * m : 128 * m + 128])

    def halos_to_parts(nat, put):
        moved = exact_dot(jnp.concatenate([nat[above_rows, :], nat[below_rows, :]], axis=0), perm_w)
        for m in range(8):
            columns = slice(128 * m, 128 * m + 128)
            put(m, -1, moved[:HALO, columns])
            put(m, 1, moved[HALO:, columns])

    rows_at = {-1: above_rows, 0: own_rows, 1: below_rows}
    h_rows_at = {-1: h_above, 0: h_own, 1: h_below}

    def put_in(ref):
        def put(m, which, value):
            ref[m, rows_at[which], :] = value

        return put

    def put_point(m, which, value):
        hist_a[0, m, h_rows_at[which], :] = value

    loads[2].wait()
    to_parts(nat_rate, put_in(rows_rate))

    mine16 = pl.ds(pl.multiple_of(16 * s, 16), 16)

    def make_coarse_rate():
        for m in range(4):
            parts = []
            for side in (0, 1):
                part = rows_rate.at[2 * m + side]
                a = part[pl.ds(HALO, 16, stride=2), :]
                parts.append(a + part[pl.ds(HALO + 1, 16, stride=2), :])
            coarse_rate[m, mine16, :] = 0.25 * (parts[0] + parts[1])

    at(is_root, make_coarse_rate)
    for t in range(n_sp):
        strip = coarse_rate.at[:, mine16, :]
        push(both(is_root, t != s), strip, strip, s_crate.at[s], j, t)

    loads[3].wait()
    to_parts(nat_src, put_in(rows_src))
    loads[4].wait()
    to_parts(nat_point, put_point)
    loads[5].wait()

    def place_initial():
        moved = exact_dot(nat_init[...], perm_w)
        for m in range(8):
            hist_c[0, m, h_own, :] = moved[:, 128 * m : 128 * m + 128]

    at(j == 0, place_initial)
    at_c = hist_c.at[0]
    push(
        both(j == 0, up),
        at_c.at[:, pl.ds(OFF + HALO, HALO), :],
        at_c.at[:, h_below, :],
        s_relax.at[2],
        j,
        s - 1,
    )
    push(
        both(j == 0, down),
        at_c.at[:, pl.ds(OFF + 32, HALO), :],
        at_c.at[:, h_above, :],
        s_relax.at[0],
        j,
        s + 1,
    )

    def fill_back(i, carry):
        o = lax.broadcasted_iota(i32, (64, 1024), 0) + 64 * i
        f = lax.broadcasted_iota(i32, (64, 1024), 1)
        hit = f == ((o & 127) << 3) + (o >> 7)
        back_w[pl.ds(pl.multiple_of(64 * i, 64), 64), :] = jnp.where(hit, 1.0, 0.0).astype(bf16)
        return carry

    def fill_join(i, carry):
        o = lax.broadcasted_iota(i32, (64, 1024), 0) + 64 * i
        f = lax.broadcasted_iota(i32, (64, 1024), 1)
        hit = (f >> 1) == ((o & 127) << 2) + (o >> 7)
        join_w[pl.ds(pl.multiple_of(64 * i, 64), 64), :] = jnp.where(hit, 1.0, 0.0).astype(bf16)
        return carry

    lax.fori_loop(0, 16, fill_back, 0)
    lax.fori_loop(0, 8, fill_join, 0)

    loads[6].wait()
    loads[7].wait()

    def add_up(i, total):
        return total + jnp.where(i < j, steps_ref[i], 0)

    start = lax.fori_loop(0, n_tm, add_up, i32(0))
    steps = steps_ref[j]

    for core, nat, other in ((first_core, nat_rate, nat_src), (second_core, nat_src, nat_rate)):
        for side, where, sem in ((up, above_rows, 0), (down, below_rows, 1)):
            cond = both(core, side)
            arrive(cond, nat.at[where, :], s_static.at[sem])
            push(cond, nat.at[where, :], nat.at[where, :], s_share.at[sem], twin, s)
    for t in range(n_sp):
        arrive(both(t != s, close(t, 1)), tiles.at[pl.ds(8 * t + 8, 8), :], s_tile.at[t])

    def block_row(b):
        strip, row = (b + 1) // 4, (b + 1) % 4
        line = tiles[pl.ds(pl.multiple_of(8 * s + 8 * strip, 8), 8), :][row : row + 1, :]
        return jnp.broadcast_to(line, (8, 128))

    for b in range(BLOCKS):
        here = block_row(b)
        safe = jnp.where(here > 0.0, here, 1.0)
        edge[b, 0] = jnp.where(sub == 0, jnp.sqrt(block_row(b - 1) * here) / safe, 1.0)
        edge[b, 1] = jnp.where(sub == 7, jnp.sqrt(block_row(b + 1) * here) / safe, 1.0)
        edge[b, 2] = jnp.where(lane == 0, 0.0, jnp.sqrt(pltpu.roll(here, 1, 1) * here) / safe)
        edge[b, 3] = jnp.where(lane == 127, 0.0, jnp.sqrt(pltpu.roll(here, 127, 1) * here) / safe)
        edge[b, 4] = here

    def weigh(blocks):
        for b in blocks:
            rows = pl.ds(8 * b, 8)
            here = edge[b, 4]
            ends = edge[b, 0] + edge[b, 1]
            for m in range(8):
                total = ends + (
                    (edge[b, 2] if m == 0 else 1.0) + (edge[b, 3] if m == 7 else 1.0)
                )
                scaled = rows_rate[m, rows, :] * here
                weight_d[m, rows, :] = scaled
                weight_e[m, rows, :] = 1.0 - scaled * total

    weigh(range(3, 7))
    for core, nat in ((first_core, nat_src), (second_core, nat_rate)):
        for side, where, sem in ((up, above_rows, 0), (down, below_rows, 1)):
            arrive(both(core, side), nat.at[where, :], s_share.at[sem])
    halos_to_parts(nat_rate, put_in(rows_rate))
    halos_to_parts(nat_src, put_in(rows_src))
    weigh((0, 1, 2, 7, 8, 9))
    arrive(up, nat_point.at[above_rows, :], s_point.at[0])
    arrive(down, nat_point.at[below_rows, :], s_point.at[1])
    halos_to_parts(nat_point, put_point)

    def half(read, write, amp, b0, b1):
        for b in range(b0, b1):
            r0 = OFF + 8 * b
            rows = pl.ds(8 * b, 8)
            cur = [read[m, pl.ds(r0, 8), :] for m in range(8)]
            far_left = pltpu.roll(cur[7], 1, 1) * edge[b, 2]
            far_right = pltpu.roll(cur[0], 127, 1) * edge[b, 3]
            for m in (1, 2, 3, 4, 5, 6, 0, 7):
                left = cur[m - 1] if m > 0 else far_left
                right = cur[m + 1] if m < 7 else far_right
                above = read[m, pl.ds(r0 - 1, 8), :] * edge[b, 0]
                below = read[m, pl.ds(r0 + 1, 8), :] * edge[b, 1]
                write[m, pl.ds(r0, 8), :] = (
                    weight_e[m, rows, :] * cur[m]
                    + weight_d[m, rows, :] * ((above + below) + (left + right))
                    + amp * rows_src[m, rows, :]
                )

    def sweep(hist):
        last = wave_ref.shape[0] - 1
        for k0, k1, b0, b1 in PLAN:

            def two_steps(k, carry, b0=b0, b1=b1):
                half(hist.at[k], hist_b.at[k], wave_ref[jnp.minimum(start + 2 * k, last)], b0, b1)
                half(
                    hist_b.at[k],
                    hist.at[k + 1],
                    wave_ref[jnp.minimum(start + 2 * k + 1, last)],
                    b0,
                    b1,
                )
                return carry

            lax.fori_loop(k0, k1, two_steps, 0)

    pair = steps >> 1
    odd_count = (steps & 1) == 1

    def state_after(hist, m, where):
        return jnp.where(odd_count, hist_b[pair, m, where, :], hist[pair, m, where, :])

    sweep(hist_a)
    for m in range(8):
        first[m] = state_after(hist_a, m, h_own)

    follow = j < n_tm - 1
    push(
        both(follow, up), first.at[:, low, :], at_c.at[:, h_below, :], s_relax.at[2], j + 1, s - 1
    )
    push(
        both(follow, down), first.at[:, high, :], at_c.at[:, h_above, :], s_relax.at[0], j + 1, s + 1
    )
    push(follow, first, at_c.at[:, h_own, :], s_relax.at[1], j + 1, s)
    def lead_setup():
        block = [tiles[pl.ds(8 + i, n_sp, stride=8), :] for i in range(4)]
        if n_sp < 8:
            rest = jnp.zeros((8 - n_sp, 128), f32)
            block = [jnp.concatenate([v, rest], axis=0) for v in block]
        for i in range(4):
            here = block[i]
            safe = jnp.where(here > 0.0, here, 1.0)
            above = block[i - 1] if i > 0 else jnp.where(sub == 0, 0.0, pltpu.roll(block[3], 1, 0))
            below = block[i + 1] if i < 3 else jnp.where(sub == 7, 0.0, pltpu.roll(block[0], 7, 0))
            side_c[0, i] = jnp.sqrt(above * here) / safe
            side_c[1, i] = jnp.sqrt(below * here) / safe
            side_c[2, i] = jnp.where(lane == 0, 0.0, jnp.sqrt(pltpu.roll(here, 1, 1) * here) / safe)
            side_c[3, i] = jnp.where(
                lane == 127, 0.0, jnp.sqrt(pltpu.roll(here, 127, 1) * here) / safe
            )
            for k in range(4 * i, 4 * i + 4):
                for m in range(4):
                    total = (
                        (side_c[0, i] if k % 4 == 0 else 1.0)
                        + (side_c[1, i] if k % 4 == 3 else 1.0)
                    ) + (
                        (side_c[2, i] if m == 0 else 1.0) + (side_c[3, i] if m == 3 else 1.0)
                    )
                    scaled = coarse_rate[m, pl.ds(k, 8, stride=16), :] * here
                    even[4 * k + m] = scaled
                    odd[4 * k + m] = scaled * total

        def one(p, carry):
            factor = steps_ref[lead_start + p].astype(f32) * (1.0 / (4.0 * CSUB))
            for v in range(64):
                weight_cd[p, v] = even[v] * factor
                weight_ce[p, v] = 1.0 - odd[v] * factor
            return carry

        lax.fori_loop(0, lead_size, one, 0)

    for t in range(n_sp):
        far = both(is_root, t != s)
        arrive(far, coarse_rate.at[:, pl.ds(16 * t, 16), :], s_crate.at[t])
        arrive(
            both(far, jnp.logical_not(close(t, 1))),
            tiles.at[pl.ds(8 * t + 8, 8), :],
            s_tile.at[t],
        )
    at(is_root, lead_setup)

    arrive(j > 0, at_c.at[:, h_own, :], s_relax.at[1])
    arrive(up, at_c.at[:, h_above, :], s_relax.at[0])
    arrive(down, at_c.at[:, h_below, :], s_relax.at[2])
    sweep(hist_c)

    for m in range(8):
        change[m] = state_after(hist_c, m, h_own) - first[m]
    for m in range(4):
        parts = []
        for side in (0, 1):
            part = change.at[2 * m + side]
            parts.append(part[pl.ds(0, 16, stride=2), :] + part[pl.ds(1, 16, stride=2), :])
        own_res[m] = 0.25 * (parts[0] + parts[1])
    slot = jnp.clip(place, 0, max(sizes) - 1)
    at(sender, lambda: pl.semaphore_wait(s_ready.at[0], 1))
    for t in range(n_sp):
        cond = both(sender, close(t, reach_res))
        push(both(cond, j > 0), own_res, res_in.at[slot, :, mine16, :], s_res.at[slot, s], root, t)
        push(both(cond, j == 0), own_res, err_in.at[:, mine16, :], s_hop.at[s], root, t)
    push(j == 0, own_res, err_own, s_err, j + 1, s)

    def residuals_in():
        def one(p, carry):
            reach = reach_of((lead_size - 1 - p) * CSUB)
            for t in range(n_sp):
                arrive(close(t, reach), res_in.at[p, :, pl.ds(16 * t, 16), :], s_res.at[p, t])
            return carry

        lax.fori_loop(0, lead_size, one, 0)

    at(is_root, residuals_in)
    for t in range(n_sp):
        arrive(
            both(is_root, close(t, reach_here)), err_in.at[:, pl.ds(16 * t, 16), :], s_hop.at[t]
        )

    def coarse_step(p, read, write, turned, turns, last):
        def row(k):
            if k == -1:
                wrapped = [pltpu.roll(read[60 + m], 1, 0) for m in range(4)]
                return [jnp.where(sub == 0, 0.0, v) for v in wrapped]
            if k == 16:
                wrapped = [pltpu.roll(read[m], 7, 0) for m in range(4)]
                return [jnp.where(sub == 7, 0.0, v) for v in wrapped]
            return [read[4 * k + m] for m in range(4)]

        above, here = None, None
        for k in range(16):
            if k == 0:
                above, here = row(-1), row(0)
            below = row(k + 1)
            i = k // 4
            for m in (0, 3, 1, 2):
                v = 4 * k + m
                left = here[m - 1] if m > 0 else turned[0, k] * side_c[2, i]
                right = here[m + 1] if m < 3 else turned[1, k] * side_c[3, i]
                high = above[m] * side_c[0, i] if k % 4 == 0 else above[m]
                deep = below[m] * side_c[1, i] if k % 4 == 3 else below[m]
                new = weight_ce[p, v] * here[m] + weight_cd[p, v] * ((high + deep) + (left + right))
                if last:
                    where = (p, m, pl.ds(k, 8, stride=16), slice(None))
                    new = new + res_in[where]
                    err_out[where] = new
                write[v] = new
                if m == 3:
                    turns[0, k] = pltpu.roll(new, 1, 1)
                if m == 0:
                    turns[1, k] = pltpu.roll(new, 127, 1)
            above, here = here, below

    def err_copy(p):
        return pltpu.make_async_remote_copy(
            src_ref=err_out.at[p, :, mine16, :],
            dst_ref=err_own,
            send_sem=s_errs.at[p],
            recv_sem=s_err,
            device_id=(lead_start + 1 + p, s),
            device_id_type=MESH,
        )

    def chain():
        for k in range(16):
            for m in range(4):
                even[4 * k + m] = err_in[m, pl.ds(k, 8, stride=16), :]
            even_turn[0, k] = pltpu.roll(even[4 * k + 3], 1, 1)
            even_turn[1, k] = pltpu.roll(even[4 * k], 127, 1)

        def two_stages(h, carry):
            p = 2 * h
            bufs = ((even, even_turn), (odd, odd_turn))
            for i in range(2 * CSUB):
                (read, turned), (write, turns) = bufs[i % 2], bufs[(i + 1) % 2]
                stage = p if i < CSUB else p + 1
                coarse_step(stage, read, write, turned, turns, i % CSUB == CSUB - 1)
                if i == CSUB - 1:
                    err_copy(p).start()
            at(p + 1 < lead_size - 1, lambda: err_copy(p + 1).start())
            return carry

        lax.fori_loop(0, lead_size // 2, two_stages, 0)

    at(is_root, chain)
    end = jnp.maximum(lead_size - 1, 0)
    at(has_next, lambda: pl.semaphore_wait(s_ready.at[1], 1))
    for t in sorted(range(n_sp), key=lambda t: -abs(2 * t - n_sp + 1)):
        push(
            both(has_next, close(t, reach_next)),
            err_out.at[end, :, mine16, :],
            err_in.at[:, mine16, :],
            s_hop.at[s],
            next_root,
            t,
        )
    at(is_root, lambda: err_copy(end).start())

    relaxed = jnp.concatenate([hist_c[0, m, h_own, :] for m in range(8)], axis=1)
    nat_rel[...] = exact_dot(relaxed, back_w)

    def no_error():
        out_ref[0] = nat_rel[...]

    def with_error():
        errors = jnp.concatenate([err_own[m] for m in range(4)], axis=1)
        spread = exact_dot(errors, join_w)
        for c in range(8):
            columns = slice(128 * c, 128 * c + 128)
            nat_err[c, pl.ds(0, 16, stride=2), :] = spread[:, columns]
            nat_err[c, pl.ds(1, 16, stride=2), :] = spread[:, columns]
            out_ref[0, :, pl.ds(128 * c, 128)] = nat_rel[:, pl.ds(128 * c, 128)] + nat_err[c]

    arrive(j > 0, err_own, s_err)
    at(j == 0, no_error)
    at(j > 0, with_error)
    for cond, make in pending:
        at(cond, lambda make=make: make().wait_send())

    def drain():
        def one(p, carry):
            err_copy(p).wait_send()
            return carry

        lax.fori_loop(0, lead_size, one, 0)

    at(is_root, drain)


def advance(dims, *args):
    n_tm, n_sp, sizes, heads = dims
    most = max(sizes)
    f32 = jnp.float32
    bf16 = jnp.bfloat16
    vm = pltpu.VMEM
    sm = pltpu.SMEM
    dma = pltpu.SemaphoreType.DMA
    hist = (STEP_MOST // 2 + 1, 8, EXT + 2 * OFF, 128)
    hbm = pl.BlockSpec(memory_space=pltpu.HBM)
    return pl.pallas_call(
        functools.partial(kernel, dims),
        out_shape=jax.ShapeDtypeStruct((1, 32, 1024), f32),
        in_specs=[hbm] * 8,
        out_specs=pl.BlockSpec(memory_space=pltpu.VMEM),
        scratch_shapes=[
            sm(args[4].shape, f32),
            sm(args[5].shape, f32),
            sm(args[6].shape, jnp.int32),
            sm(args[7].shape, jnp.int32),
            vm((EXT, 1024), f32),
            vm((EXT, 1024), f32),
            vm((EXT, 1024), f32),
            vm((32, 1024), f32),
            vm(hist, f32),
            vm(hist, f32),
            vm(hist, f32),
            vm((8, EXT, 128), f32),
            vm((8, EXT, 128), f32),
            vm((8, EXT, 128), f32),
            vm((8, EXT, 128), f32),
            vm((BLOCKS, 5, 8, 128), f32),
            vm((8 * (n_sp + 2), 128), f32),
            vm((8, 32, 128), f32),
            vm((8, 32, 128), f32),
            vm((1024, 1024), bf16),
            vm((1024, 1024), bf16),
            vm((512, 1024), bf16),
            vm((4, 16, 128), f32),
            vm((4, 128, 128), f32),
            vm((most, 4, 128, 128), f32),
            vm((4, 128, 128), f32),
            vm((most, 64, 8, 128), f32),
            vm((most, 64, 8, 128), f32),
            vm((4, 4, 8, 128), f32),
            vm((64, 8, 128), f32),
            vm((64, 8, 128), f32),
            vm((2, 16, 8, 128), f32),
            vm((2, 16, 8, 128), f32),
            vm((most, 4, 128, 128), f32),
            vm((4, 16, 128), f32),
            vm((32, 1024), f32),
            vm((8, 32, 128), f32),
            pltpu.SemaphoreType.REGULAR((2,)),
            dma((8,)),
            dma((72,)),
            dma((most,)),
            dma((2,)),
            dma((2,)),
            dma((2,)),
            dma((8,)),
            dma((8,)),
            dma((3,)),
            dma((most, 8)),
            dma((8,)),
            dma(()),
        ],
        compiler_params=pltpu.CompilerParams(
            collective_id=0, has_side_effects=True, vmem_limit_bytes=66846720
        ),
    )(*args)


def solution(mesh, sizes=GROUPS, heads=LEADS):
    placed = (
        P("tm", "space", None),
        P("space", None),
        P("space", None),
        P("space", None),
        P(),
        P(),
        P("space", None),
        P(),
    )
    dims = (mesh.shape["tm"], mesh.shape["space"], sizes, heads)
    return jax.shard_map(
        functools.partial(advance, dims),
        mesh=mesh,
        in_specs=placed,
        out_specs=P("tm", "space", None),
        check_vma=False,
    )
```

```python
import functools

import jax
import jax.numpy as jnp
from jax import lax
from jax.experimental import pallas as pl
from jax.experimental.pallas import tpu as pltpu
from jax.sharding import PartitionSpec as P

MESH = pl.DeviceIdType.MESH
STEP_MOST = 20
CSUB = 5
HALO = 24
EXT = 32 + 2 * HALO
OFF = 8
BLOCKS = EXT // 8
PLAN = ((0, 2, 0, 10), (2, 6, 1, 9), (6, 10, 2, 8))
GROUPS = (4, 12, 14)
LEADS = (6, 4, 12)


def kernel(
    dims,
    point_ref,
    init_ref,
    rate_ref,
    src_ref,
    wave_hbm,
    table_hbm,
    class_hbm,
    steps_hbm,
    out_ref,
    wave_ref,
    table_ref,
    class_ref,
    steps_ref,
    nat_point,
    nat_rate,
    nat_src,
    nat_init,
    hist_a,
    hist_b,
    hist_c,
    rows_rate,
    rows_src,
    weight_d,
    weight_e,
    edge,
    tiles,
    first,
    change,
    perm_w,
    back_w,
    join_w,
    own_res,
    coarse_rate,
    res_in,
    err_in,
    weight_cd,
    weight_ce,
    side_c,
    even,
    odd,
    even_turn,
    odd_turn,
    err_out,
    err_own,
    nat_rel,
    nat_err,
    s_ready,
    s_local,
    s_send,
    s_errs,
    s_point,
    s_static,
    s_share,
    s_tile,
    s_crate,
    s_relax,
    s_res,
    s_hop,
    s_err,
):
    n_tm, n_sp, sizes, heads = dims
    groups = len(sizes)
    starts_of = [1 + sum(sizes[:g]) for g in range(groups + 1)]
    f32 = jnp.float32
    bf16 = jnp.bfloat16
    i32 = jnp.int32
    j = lax.axis_index("tm")
    s = lax.axis_index("space")
    twin = j + 1 - 2 * (j % 2)
    pending = []

    def at(cond, body):
        pl.when(cond)(body)

    def both(a, b):
        return jnp.logical_and(a, b)

    def pick(values, index):
        out = i32(values[0])
        for g in range(1, len(values)):
            out = jnp.where(index == g, i32(values[g]), out)
        return out

    def reach_of(rows):
        return (rows + 15) // 16

    def close(t, reach):
        return both(t - s <= reach, s - t <= reach)

    group = i32(0)
    out_group = i32(0)
    for g in range(1, groups):
        group = group + (j >= starts_of[g]).astype(i32)
        out_group = out_group + (j >= starts_of[g] + 1).astype(i32)
    sender = j < starts_of[groups]
    place = j - pick(starts_of, group)
    root = pick(heads, group)
    reach_res = jnp.where(
        j == 0, reach_of(CSUB * sizes[0]), reach_of((pick(sizes, group) - 1 - place) * CSUB)
    )
    is_root = jnp.bool_(False)
    lead = i32(0)
    for g in range(groups):
        is_root = jnp.logical_or(is_root, j == heads[g])
        lead = lead + jnp.where(j == heads[g], g, 0)
    lead_size = pick(sizes, lead)
    lead_start = pick(starts_of, lead)
    has_next = both(is_root, lead < groups - 1)
    next_lead = jnp.minimum(lead + 1, groups - 1)
    next_root = pick(heads, next_lead)
    reach_next = reach_of(CSUB * pick(sizes, next_lead))
    reach_here = reach_of(CSUB * lead_size)

    top, bottom = s == 0, s == n_sp - 1
    up, down = s > 0, s < n_sp - 1

    loads = [
        pltpu.make_async_copy(class_hbm, class_ref, s_local.at[0]),
        pltpu.make_async_copy(table_hbm, table_ref, s_local.at[1]),
        pltpu.make_async_copy(rate_ref, nat_rate.at[pl.ds(HALO, 32), :], s_local.at[2]),
        pltpu.make_async_copy(src_ref, nat_src.at[pl.ds(HALO, 32), :], s_local.at[3]),
        pltpu.make_async_copy(point_ref.at[0], nat_point.at[pl.ds(HALO, 32), :], s_local.at[4]),
        pltpu.make_async_copy(init_ref, nat_init, s_local.at[5]),
        pltpu.make_async_copy(steps_hbm, steps_ref, s_local.at[6]),
        pltpu.make_async_copy(wave_hbm, wave_ref, s_local.at[7]),
    ]
    for load in loads:
        load.start()

    barrier = pltpu.get_barrier_semaphore()
    expect = i32(1)

    def signal(tm, sp):
        pl.semaphore_signal(barrier, inc=1, device_id=(tm, sp), device_id_type=MESH)

    def tell(cond, tm, sp):
        at(cond, lambda: signal(tm, sp))

    tell(sender, root, s)
    tell(j >= 2, pick(heads, out_group), s)
    tell(has_next, next_root, s)
    signal(twin, s)
    for t in range(n_sp):
        beside = both(t != s, jnp.logical_or(is_root, close(t, 1)))
        tell(beside, j, t)
        tell(both(j > 0, close(t, 1)), j - 1, t)
        expect = expect + beside.astype(i32)
        expect = expect + both(j < n_tm - 1, close(t, 1)).astype(i32)
    expect = expect + jnp.where(is_root, 2 * lead_size + 1, 0)

    count = [0]

    def push(cond, src, dst, sem, tm, sp):
        slot = count[0]
        count[0] += 1

        def make():
            return pltpu.make_async_remote_copy(
                src_ref=src,
                dst_ref=dst,
                send_sem=s_send.at[slot],
                recv_sem=sem,
                device_id=(tm, sp),
                device_id_type=MESH,
            )

        at(cond, lambda: make().start())
        pending.append((cond, make))

    def arrive(cond, dst, sem):
        def body():
            pltpu.make_async_remote_copy(
                src_ref=dst,
                dst_ref=dst,
                send_sem=s_send.at[0],
                recv_sem=sem,
                device_id=(j, s),
                device_id_type=MESH,
            ).wait_recv()

        at(cond, body)

    sub = lax.broadcasted_iota(i32, (8, 128), 0)
    lane = lax.broadcasted_iota(i32, (8, 128), 1)
    above_rows, own_rows, below_rows = pl.ds(0, HALO), pl.ds(HALO, 32), pl.ds(HALO + 32, HALO)
    h_above, h_own, h_below = pl.ds(OFF, HALO), pl.ds(OFF + HALO, 32), pl.ds(OFF + HALO + 32, HALO)

    def clear(where, h_where, tile):
        for buf in (nat_point, nat_rate, nat_src):
            buf[where, :] = jnp.zeros((HALO, 1024), f32)
        hist_c[0, :, h_where, :] = jnp.zeros((8, HALO, 128), f32)
        tiles[pl.ds(8 * tile, 8), :] = jnp.zeros((8, 128), f32)

    at(top, lambda: clear(above_rows, h_above, 0))
    at(bottom, lambda: clear(below_rows, h_below, n_sp + 1))

    loads[0].wait()
    loads[1].wait()
    tile = jnp.zeros((8, 128), f32)
    for i in range(4):
        for c in range(8):
            tile = jnp.where(both(sub == i, lane // 16 == c), table_ref[class_ref[i, c]], tile)
    my_tile = tiles.at[pl.ds(pl.multiple_of(8 * s + 8, 8), 8), :]
    my_tile[...] = tile

    def fill_perm(i, carry):
        f = lax.broadcasted_iota(i32, (64, 1024), 0) + 64 * i
        o = lax.broadcasted_iota(i32, (64, 1024), 1)
        hit = o == ((f & 7) << 7) + (f >> 3)
        perm_w[pl.ds(pl.multiple_of(64 * i, 64), 64), :] = jnp.where(hit, 1.0, 0.0).astype(bf16)
        return carry

    lax.fori_loop(0, 16, fill_perm, 0)

    pl.semaphore_wait(barrier, expect)

    for t in range(n_sp):
        push(
            both(t != s, jnp.logical_or(is_root, close(t, 1))), my_tile, my_tile, s_tile.at[s], j, t
        )
    low, high = pl.ds(0, HALO), pl.ds(32 - HALO, HALO)
    first_core, second_core = j % 2 == 0, j % 2 == 1
    for core, ref, nat in ((first_core, rate_ref, nat_rate), (second_core, src_ref, nat_src)):
        push(both(core, up), ref.at[low, :], nat.at[below_rows, :], s_static.at[1], j, s - 1)
        push(both(core, down), ref.at[high, :], nat.at[above_rows, :], s_static.at[0], j, s + 1)
    push(up, point_ref.at[0, low, :], nat_point.at[below_rows, :], s_point.at[1], j, s - 1)
    push(down, point_ref.at[0, high, :], nat_point.at[above_rows, :], s_point.at[0], j, s + 1)

    def answer():
        def ready(which, tm):
            pl.semaphore_signal(
                s_ready.at[which], inc=1, device_id=(tm, s), device_id_type=MESH
            )

        def one(p, carry):
            ready(0, lead_start + p)
            return carry

        lax.fori_loop(0, lead_size, one, 0)
        at(lead == 0, lambda: ready(0, 0))
        at(lead > 0, lambda: ready(1, pick(heads, jnp.maximum(lead - 1, 0))))

    at(is_root, answer)

    def exact_dot(values, matrix):
        large = values.astype(bf16)
        rest = values - large.astype(f32)
        mid = rest.astype(bf16)
        small = (rest - mid.astype(f32)).astype(bf16)
        n = values.shape[0]
        parts = jnp.dot(
            jnp.concatenate([large, mid, small], axis=0), matrix[...], preferred_element_type=f32
        )
        return (parts[2 * n :] + parts[n : 2 * n]) + parts[:n]

    def to_parts(nat, put):
        moved = exact_dot(nat[own_rows, :], perm_w)
        for m in range(8):
            put(m, 0, moved[:, 128 * m : 128 * m + 128])

    def halos_to_parts(nat, put):
        moved = exact_dot(jnp.concatenate([nat[above_rows, :], nat[below_rows, :]], axis=0), perm_w)
        for m in range(8):
            columns = slice(128 * m, 128 * m + 128)
            put(m, -1, moved[:HALO, columns])
            put(m, 1, moved[HALO:, columns])

    rows_at = {-1: above_rows, 0: own_rows, 1: below_rows}
    h_rows_at = {-1: h_above, 0: h_own, 1: h_below}

    def put_in(ref):
        def put(m, which, value):
            ref[m, rows_at[which], :] = value

        return put

    def put_point(m, which, value):
        hist_a[0, m, h_rows_at[which], :] = value

    loads[2].wait()
    to_parts(nat_rate, put_in(rows_rate))

    mine16 = pl.ds(pl.multiple_of(16 * s, 16), 16)

    def make_coarse_rate():
        for m in range(4):
            parts = []
            for side in (0, 1):
                part = rows_rate.at[2 * m + side]
                a = part[pl.ds(HALO, 16, stride=2), :]
                parts.append(a + part[pl.ds(HALO + 1, 16, stride=2), :])
            coarse_rate[m, mine16, :] = 0.25 * (parts[0] + parts[1])

    at(is_root, make_coarse_rate)
    for t in range(n_sp):
        strip = coarse_rate.at[:, mine16, :]
        push(both(is_root, t != s), strip, strip, s_crate.at[s], j, t)

    loads[3].wait()
    to_parts(nat_src, put_in(rows_src))
    loads[4].wait()
    to_parts(nat_point, put_point)
    loads[5].wait()

    def place_initial():
        moved = exact_dot(nat_init[...], perm_w)
        for m in range(8):
            hist_c[0, m, h_own, :] = moved[:, 128 * m : 128 * m + 128]

    at(j == 0, place_initial)
    at_c = hist_c.at[0]
    push(
        both(j == 0, up),
        at_c.at[:, pl.ds(OFF + HALO, HALO), :],
        at_c.at[:, h_below, :],
        s_relax.at[2],
        j,
        s - 1,
    )
    push(
        both(j == 0, down),
        at_c.at[:, pl.ds(OFF + 32, HALO), :],
        at_c.at[:, h_above, :],
        s_relax.at[0],
        j,
        s + 1,
    )

    def fill_back(i, carry):
        o = lax.broadcasted_iota(i32, (64, 1024), 0) + 64 * i
        f = lax.broadcasted_iota(i32, (64, 1024), 1)
        hit = f == ((o & 127) << 3) + (o >> 7)
        back_w[pl.ds(pl.multiple_of(64 * i, 64), 64), :] = jnp.where(hit, 1.0, 0.0).astype(bf16)
        return carry

    def fill_join(i, carry):
        o = lax.broadcasted_iota(i32, (64, 1024), 0) + 64 * i
        f = lax.broadcasted_iota(i32, (64, 1024), 1)
        hit = (f >> 1) == ((o & 127) << 2) + (o >> 7)
        join_w[pl.ds(pl.multiple_of(64 * i, 64), 64), :] = jnp.where(hit, 1.0, 0.0).astype(bf16)
        return carry


    loads[6].wait()
    loads[7].wait()

    def add_up(i, total):
        return total + jnp.where(i < j, steps_ref[i], 0)

    start = lax.fori_loop(0, n_tm, add_up, i32(0))
    steps = steps_ref[j]

    for core, nat, other in ((first_core, nat_rate, nat_src), (second_core, nat_src, nat_rate)):
        for side, where, sem in ((up, above_rows, 0), (down, below_rows, 1)):
            cond = both(core, side)
            arrive(cond, nat.at[where, :], s_static.at[sem])
            push(cond, nat.at[where, :], nat.at[where, :], s_share.at[sem], twin, s)
    for t in range(n_sp):
        arrive(both(t != s, close(t, 1)), tiles.at[pl.ds(8 * t + 8, 8), :], s_tile.at[t])

    def block_row(b):
        strip, row = (b + 1) // 4, (b + 1) % 4
        line = tiles[pl.ds(pl.multiple_of(8 * s + 8 * strip, 8), 8), :][row : row + 1, :]
        return jnp.broadcast_to(line, (8, 128))

    for b in range(BLOCKS):
        here = block_row(b)
        safe = jnp.where(here > 0.0, here, 1.0)
        edge[b, 0] = jnp.where(sub == 0, jnp.sqrt(block_row(b - 1) * here) / safe, 1.0)
        edge[b, 1] = jnp.where(sub == 7, jnp.sqrt(block_row(b + 1) * here) / safe, 1.0)
        edge[b, 2] = jnp.where(lane == 0, 0.0, jnp.sqrt(pltpu.roll(here, 1, 1) * here) / safe)
        edge[b, 3] = jnp.where(lane == 127, 0.0, jnp.sqrt(pltpu.roll(here, 127, 1) * here) / safe)
        edge[b, 4] = here

    def weigh(blocks):
        for b in blocks:
            rows = pl.ds(8 * b, 8)
            here = edge[b, 4]
            ends = edge[b, 0] + edge[b, 1]
            for m in range(8):
                total = ends + (
                    (edge[b, 2] if m == 0 else 1.0) + (edge[b, 3] if m == 7 else 1.0)
                )
                scaled = rows_rate[m, rows, :] * here
                weight_d[m, rows, :] = scaled
                weight_e[m, rows, :] = 1.0 - scaled * total

    weigh(range(3, 7))
    at(first_core, lambda: halos_to_parts(nat_rate, put_in(rows_rate)))
    at(second_core, lambda: halos_to_parts(nat_src, put_in(rows_src)))
    for core, nat in ((first_core, nat_src), (second_core, nat_rate)):
        for side, where, sem in ((up, above_rows, 0), (down, below_rows, 1)):
            arrive(both(core, side), nat.at[where, :], s_share.at[sem])
    at(second_core, lambda: halos_to_parts(nat_rate, put_in(rows_rate)))
    at(first_core, lambda: halos_to_parts(nat_src, put_in(rows_src)))
    weigh((0, 1, 2, 7, 8, 9))
    arrive(up, nat_point.at[above_rows, :], s_point.at[0])
    arrive(down, nat_point.at[below_rows, :], s_point.at[1])
    halos_to_parts(nat_point, put_point)

    def half(read, write, amp, b0, b1):
        for b in range(b0, b1):
            r0 = OFF + 8 * b
            rows = pl.ds(8 * b, 8)
            cur = [read[m, pl.ds(r0, 8), :] for m in range(8)]
            far_left = pltpu.roll(cur[7], 1, 1) * edge[b, 2]
            far_right = pltpu.roll(cur[0], 127, 1) * edge[b, 3]
            for m in (1, 2, 3, 4, 5, 6, 0, 7):
                left = cur[m - 1] if m > 0 else far_left
                right = cur[m + 1] if m < 7 else far_right
                above = read[m, pl.ds(r0 - 1, 8), :] * edge[b, 0]
                below = read[m, pl.ds(r0 + 1, 8), :] * edge[b, 1]
                write[m, pl.ds(r0, 8), :] = (
                    weight_e[m, rows, :] * cur[m]
                    + weight_d[m, rows, :] * ((above + below) + (left + right))
                    + amp * rows_src[m, rows, :]
                )

    def sweep(hist):
        last = wave_ref.shape[0] - 1
        for k0, k1, b0, b1 in PLAN:

            def two_steps(k, carry, b0=b0, b1=b1):
                half(hist.at[k], hist_b.at[k], wave_ref[jnp.minimum(start + 2 * k, last)], b0, b1)
                half(
                    hist_b.at[k],
                    hist.at[k + 1],
                    wave_ref[jnp.minimum(start + 2 * k + 1, last)],
                    b0,
                    b1,
                )
                return carry

            lax.fori_loop(k0, k1, two_steps, 0)

    pair = steps >> 1
    odd_count = (steps & 1) == 1

    def state_after(hist, m, where):
        return jnp.where(odd_count, hist_b[pair, m, where, :], hist[pair, m, where, :])

    sweep(hist_a)
    for m in range(8):
        first[m] = state_after(hist_a, m, h_own)

    follow = j < n_tm - 1
    push(
        both(follow, up), first.at[:, low, :], at_c.at[:, h_below, :], s_relax.at[2], j + 1, s - 1
    )
    push(
        both(follow, down), first.at[:, high, :], at_c.at[:, h_above, :], s_relax.at[0], j + 1, s + 1
    )
    push(follow, first, at_c.at[:, h_own, :], s_relax.at[1], j + 1, s)
    def lead_setup():
        block = [tiles[pl.ds(8 + i, n_sp, stride=8), :] for i in range(4)]
        if n_sp < 8:
            rest = jnp.zeros((8 - n_sp, 128), f32)
            block = [jnp.concatenate([v, rest], axis=0) for v in block]
        for i in range(4):
            here = block[i]
            safe = jnp.where(here > 0.0, here, 1.0)
            above = block[i - 1] if i > 0 else jnp.where(sub == 0, 0.0, pltpu.roll(block[3], 1, 0))
            below = block[i + 1] if i < 3 else jnp.where(sub == 7, 0.0, pltpu.roll(block[0], 7, 0))
            side_c[0, i] = jnp.sqrt(above * here) / safe
            side_c[1, i] = jnp.sqrt(below * here) / safe
            side_c[2, i] = jnp.where(lane == 0, 0.0, jnp.sqrt(pltpu.roll(here, 1, 1) * here) / safe)
            side_c[3, i] = jnp.where(
                lane == 127, 0.0, jnp.sqrt(pltpu.roll(here, 127, 1) * here) / safe
            )
            for k in range(4 * i, 4 * i + 4):
                for m in range(4):
                    total = (
                        (side_c[0, i] if k % 4 == 0 else 1.0)
                        + (side_c[1, i] if k % 4 == 3 else 1.0)
                    ) + (
                        (side_c[2, i] if m == 0 else 1.0) + (side_c[3, i] if m == 3 else 1.0)
                    )
                    scaled = coarse_rate[m, pl.ds(k, 8, stride=16), :] * here
                    even[4 * k + m] = scaled
                    odd[4 * k + m] = scaled * total

        def one(p, carry):
            factor = steps_ref[lead_start + p].astype(f32) * (1.0 / (4.0 * CSUB))
            for v in range(64):
                weight_cd[p, v] = even[v] * factor
                weight_ce[p, v] = 1.0 - odd[v] * factor
            return carry

        lax.fori_loop(0, lead_size, one, 0)

    for t in range(n_sp):
        far = both(is_root, t != s)
        arrive(far, coarse_rate.at[:, pl.ds(16 * t, 16), :], s_crate.at[t])
        arrive(
            both(far, jnp.logical_not(close(t, 1))),
            tiles.at[pl.ds(8 * t + 8, 8), :],
            s_tile.at[t],
        )
    at(is_root, lead_setup)

    lax.fori_loop(0, 16, fill_back, 0)
    lax.fori_loop(0, 8, fill_join, 0)
    arrive(j > 0, at_c.at[:, h_own, :], s_relax.at[1])
    arrive(up, at_c.at[:, h_above, :], s_relax.at[0])
    arrive(down, at_c.at[:, h_below, :], s_relax.at[2])
    sweep(hist_c)

    for m in range(8):
        change[m] = state_after(hist_c, m, h_own) - first[m]
    for m in range(4):
        parts = []
        for side in (0, 1):
            part = change.at[2 * m + side]
            parts.append(part[pl.ds(0, 16, stride=2), :] + part[pl.ds(1, 16, stride=2), :])
        own_res[m] = 0.25 * (parts[0] + parts[1])
    slot = jnp.clip(place, 0, max(sizes) - 1)
    at(sender, lambda: pl.semaphore_wait(s_ready.at[0], 1))
    for t in range(n_sp):
        cond = both(sender, close(t, reach_res))
        push(both(cond, j > 0), own_res, res_in.at[slot, :, mine16, :], s_res.at[slot, s], root, t)
        push(both(cond, j == 0), own_res, err_in.at[:, mine16, :], s_hop.at[s], root, t)
    push(j == 0, own_res, err_own, s_err, j + 1, s)

    def residuals_in():
        def one(p, carry):
            reach = reach_of((lead_size - 1 - p) * CSUB)
            for t in range(n_sp):
                arrive(close(t, reach), res_in.at[p, :, pl.ds(16 * t, 16), :], s_res.at[p, t])
            return carry

        lax.fori_loop(0, lead_size, one, 0)

    at(is_root, residuals_in)
    for t in range(n_sp):
        arrive(
            both(is_root, close(t, reach_here)), err_in.at[:, pl.ds(16 * t, 16), :], s_hop.at[t]
        )

    def coarse_step(p, read, write, turned, turns, last):
        def row(k):
            if k == -1:
                wrapped = [pltpu.roll(read[60 + m], 1, 0) for m in range(4)]
                return [jnp.where(sub == 0, 0.0, v) for v in wrapped]
            if k == 16:
                wrapped = [pltpu.roll(read[m], 7, 0) for m in range(4)]
                return [jnp.where(sub == 7, 0.0, v) for v in wrapped]
            return [read[4 * k + m] for m in range(4)]

        above, here = None, None
        for k in range(16):
            if k == 0:
                above, here = row(-1), row(0)
            below = row(k + 1)
            i = k // 4
            for m in (0, 3, 1, 2):
                v = 4 * k + m
                left = here[m - 1] if m > 0 else turned[0, k] * side_c[2, i]
                right = here[m + 1] if m < 3 else turned[1, k] * side_c[3, i]
                high = above[m] * side_c[0, i] if k % 4 == 0 else above[m]
                deep = below[m] * side_c[1, i] if k % 4 == 3 else below[m]
                new = weight_ce[p, v] * here[m] + weight_cd[p, v] * ((high + deep) + (left + right))
                if last:
                    where = (p, m, pl.ds(k, 8, stride=16), slice(None))
                    new = new + res_in[where]
                    err_out[where] = new
                write[v] = new
                if m == 3:
                    turns[0, k] = pltpu.roll(new, 1, 1)
                if m == 0:
                    turns[1, k] = pltpu.roll(new, 127, 1)
            above, here = here, below

    def err_copy(p):
        return pltpu.make_async_remote_copy(
            src_ref=err_out.at[p, :, mine16, :],
            dst_ref=err_own,
            send_sem=s_errs.at[p],
            recv_sem=s_err,
            device_id=(lead_start + 1 + p, s),
            device_id_type=MESH,
        )

    def chain():
        for k in range(16):
            for m in range(4):
                even[4 * k + m] = err_in[m, pl.ds(k, 8, stride=16), :]
            even_turn[0, k] = pltpu.roll(even[4 * k + 3], 1, 1)
            even_turn[1, k] = pltpu.roll(even[4 * k], 127, 1)

        def two_stages(h, carry):
            p = 2 * h
            bufs = ((even, even_turn), (odd, odd_turn))
            for i in range(2 * CSUB):
                (read, turned), (write, turns) = bufs[i % 2], bufs[(i + 1) % 2]
                stage = p if i < CSUB else p + 1
                coarse_step(stage, read, write, turned, turns, i % CSUB == CSUB - 1)
                if i == CSUB - 1:
                    err_copy(p).start()
            at(p + 1 < lead_size - 1, lambda: err_copy(p + 1).start())
            return carry

        lax.fori_loop(0, lead_size // 2, two_stages, 0)

    at(is_root, chain)
    end = jnp.maximum(lead_size - 1, 0)
    at(has_next, lambda: pl.semaphore_wait(s_ready.at[1], 1))
    for t in sorted(range(n_sp), key=lambda t: -abs(2 * t - n_sp + 1)):
        push(
            both(has_next, close(t, reach_next)),
            err_out.at[end, :, mine16, :],
            err_in.at[:, mine16, :],
            s_hop.at[s],
            next_root,
            t,
        )
    at(is_root, lambda: err_copy(end).start())

    relaxed = jnp.concatenate([hist_c[0, m, h_own, :] for m in range(8)], axis=1)
    nat_rel[...] = exact_dot(relaxed, back_w)

    def no_error():
        out_ref[0] = nat_rel[...]

    def with_error():
        errors = jnp.concatenate([err_own[m] for m in range(4)], axis=1)
        spread = exact_dot(errors, join_w)
        for c in range(8):
            columns = slice(128 * c, 128 * c + 128)
            nat_err[c, pl.ds(0, 16, stride=2), :] = spread[:, columns]
            nat_err[c, pl.ds(1, 16, stride=2), :] = spread[:, columns]
            out_ref[0, :, pl.ds(128 * c, 128)] = nat_rel[:, pl.ds(128 * c, 128)] + nat_err[c]

    arrive(j > 0, err_own, s_err)
    at(j == 0, no_error)
    at(j > 0, with_error)
    for cond, make in pending:
        at(cond, lambda make=make: make().wait_send())

    def drain():
        def one(p, carry):
            err_copy(p).wait_send()
            return carry

        lax.fori_loop(0, lead_size, one, 0)

    at(is_root, drain)


def advance(dims, *args):
    n_tm, n_sp, sizes, heads = dims
    most = max(sizes)
    f32 = jnp.float32
    bf16 = jnp.bfloat16
    vm = pltpu.VMEM
    sm = pltpu.SMEM
    dma = pltpu.SemaphoreType.DMA
    hist = (STEP_MOST // 2 + 1, 8, EXT + 2 * OFF, 128)
    hbm = pl.BlockSpec(memory_space=pltpu.HBM)
    return pl.pallas_call(
        functools.partial(kernel, dims),
        out_shape=jax.ShapeDtypeStruct((1, 32, 1024), f32),
        in_specs=[hbm] * 8,
        out_specs=pl.BlockSpec(memory_space=pltpu.VMEM),
        scratch_shapes=[
            sm(args[4].shape, f32),
            sm(args[5].shape, f32),
            sm(args[6].shape, jnp.int32),
            sm(args[7].shape, jnp.int32),
            vm((EXT, 1024), f32),
            vm((EXT, 1024), f32),
            vm((EXT, 1024), f32),
            vm((32, 1024), f32),
            vm(hist, f32),
            vm(hist, f32),
            vm(hist, f32),
            vm((8, EXT, 128), f32),
            vm((8, EXT, 128), f32),
            vm((8, EXT, 128), f32),
            vm((8, EXT, 128), f32),
            vm((BLOCKS, 5, 8, 128), f32),
            vm((8 * (n_sp + 2), 128), f32),
            vm((8, 32, 128), f32),
            vm((8, 32, 128), f32),
            vm((1024, 1024), bf16),
            vm((1024, 1024), bf16),
            vm((512, 1024), bf16),
            vm((4, 16, 128), f32),
            vm((4, 128, 128), f32),
            vm((most, 4, 128, 128), f32),
            vm((4, 128, 128), f32),
            vm((most, 64, 8, 128), f32),
            vm((most, 64, 8, 128), f32),
            vm((4, 4, 8, 128), f32),
            vm((64, 8, 128), f32),
            vm((64, 8, 128), f32),
            vm((2, 16, 8, 128), f32),
            vm((2, 16, 8, 128), f32),
            vm((most, 4, 128, 128), f32),
            vm((4, 16, 128), f32),
            vm((32, 1024), f32),
            vm((8, 32, 128), f32),
            pltpu.SemaphoreType.REGULAR((2,)),
            dma((8,)),
            dma((72,)),
            dma((most,)),
            dma((2,)),
            dma((2,)),
            dma((2,)),
            dma((8,)),
            dma((8,)),
            dma((3,)),
            dma((most, 8)),
            dma((8,)),
            dma(()),
        ],
        compiler_params=pltpu.CompilerParams(
            collective_id=0, has_side_effects=True, vmem_limit_bytes=66846720
        ),
    )(*args)


def solution(mesh, sizes=GROUPS, heads=LEADS):
    placed = (
        P("tm", "space", None),
        P("space", None),
        P("space", None),
        P("space", None),
        P(),
        P(),
        P("space", None),
        P(),
    )
    dims = (mesh.shape["tm"], mesh.shape["space"], sizes, heads)
    return jax.shard_map(
        functools.partial(advance, dims),
        mesh=mesh,
        in_specs=placed,
        out_specs=P("tm", "space", None),
        check_vma=False,
    )
```
